128 devices in a mesh: dom: 32 (over y, z, core), tm: 4 (over x).
Axes of the slice: x: 4, y: 4, z: 4, core: 2. Of those that a mesh axis runs over, the one named last changes fastest.
Arguments:
- panel_signal: bfloat16 [8, 32768], P('tm', 'dom'), may hold values from -6 to 6
- panel_box: int32 [32768], P('dom'), may hold values from 0 to 15
- radiation: bfloat16 [32768, 1024], P('dom'), may hold values from -0.75 to 0.75
- reception: bfloat16 [32768, 1024], P('dom'), may hold values from -0.1875 to 0.1875
- translation: bfloat16 [64, 8, 1024], P(None, None, 'dom'), may hold values from -1 to 1
- list_source: int32 [512, 8], replicated, may hold values from 0 to 511
- list_class: int32 [512, 8], replicated, may hold values from 0 to 63
- list_count: int32 [512], replicated, may hold values from 1 to 8, as said below
Outputs:
- panel_field: bfloat16 [8, 32768], P('tm', 'dom')
The draws below stay inside these ranges and needn't reach their ends.
Inputs may be any that keep to these rules, and one draw needn't show every extreme that they name: `panel_box`: indices a panel's box among the 16 boxes of its own index of dom. Box a uses the first list_count[a] entries of its lists; the rest are padding.
All inputs are finite; a program needn't handle non-finite values.
Results may differ from the reference program's by a relative error of at most 0.0057.
Values may be sent and summed in bfloat16 or wider, within the bound.
No kernel may reach another device: no remote copies, remote signals or barrier semaphores. Data moves between devices by JAX's collectives and lax.ppermute only.
A program may use at most 64 MiB of HBM per device.

```python
import math
import jax
import jax.numpy as jnp
import numpy as np
from jax import lax

K = 1024
PAN_DEV = 1024
BOX_DEV = 16
J = 8
C = 64
TS = 8
B = 512
PAN = 32768
N_DOM = 32


def draw_list_count(key, part):
    counts = jax.random.randint(jax.random.fold_in(key, 7), (B,), 1, J + 1)
    return counts.at[0].set(J).astype(jnp.int32)


def with_ends(values, key, low, largest):
    spot = [jax.random.randint(jax.random.fold_in(key, axis), (), 0, length) for axis, length in enumerate(values.shape)]
    widest = values.shape.index(max(values.shape))
    next_to = spot[:widest] + [(spot[widest] + 1) % values.shape[widest]] + spot[widest + 1:]
    return values.at[tuple(spot)].set(low).at[tuple(next_to)].set(largest)


def levels(rng, shape, cuts, least, largest):
    def one(dim, parts):
        steps = jax.random.uniform(jax.random.fold_in(jax.random.fold_in(rng, 6), dim), (parts,), jnp.float32, least / len(cuts), largest / len(cuts))
        return jnp.repeat(jnp.exp(steps), shape[dim] // parts).reshape((-1,) + (1,) * (len(shape) - dim - 1))

    factor_of = one(*cuts[0])
    for cut in cuts[1:]:
        factor_of = factor_of * one(*cut)
    return factor_of


def rank_table(number_of, skew):
    portions = [(1 << 20) // math.isqrt(standing ** skew) + 1 for standing in range(1, number_of + 1)]
    spread = 1 + sum(portions) // (1 << 30)
    return np.cumsum(np.array([max(1, weight // spread) for weight in portions]))


def ranked(own_key, extent, count, lean):
    table = rank_table(count, lean)
    pick = jax.random.randint(jax.random.fold_in(own_key, 1), extent, 0, int(table[count - 1]))
    grade = jnp.searchsorted(jnp.asarray(table, jnp.int32), pick, side="right")
    return jax.random.permutation(jax.random.fold_in(own_key, 2), count)[grade].astype(jnp.int32)


def gaussian(key, dims, scale, limit, shards=(), kind=jnp.bfloat16):
    drawn = jax.random.normal(key, dims, jnp.float32) * scale
    if len(shards) > 0:
        drawn = levels(key, dims, shards, -0.22, 0.18) * drawn
    return jnp.clip(drawn, min=-limit, max=limit).astype(kind)


def setup_inputs(seed: int = 0) -> dict:
    key_of = jax.random.split(jax.random.key(seed), 9)
    panel_signal = gaussian(key_of[0], (TS, PAN), 1.0, 6.0, ((0, 4), (1, 32)))
    panel_box = with_ends(ranked(key_of[1], (PAN,), BOX_DEV, 2), jax.random.fold_in(key_of[1], 3), 0, BOX_DEV - 1).astype(jnp.int32)
    radiation = gaussian(key_of[2], (PAN, K), (PAN_DEV // BOX_DEV) ** -0.5, 0.75, ((0, 32),))
    reception = gaussian(key_of[3], (PAN, K), K ** -0.5, 0.1875, ((0, 32),))
    translation = gaussian(key_of[4], (C, TS, K), (J * TS // 2) ** -0.5, 1.0, ((2, 32),))
    list_source = with_ends(jax.random.randint(key_of[5], (B, J), 0, B), jax.random.fold_in(key_of[5], 1), 0, B - 1).astype(jnp.int32)
    list_class = with_ends(jax.random.randint(key_of[6], (B, J), 0, C), jax.random.fold_in(key_of[6], 1), 0, C - 1).astype(jnp.int32)
    list_count = draw_list_count(jax.random.fold_in(key_of[8], 71), 0)
    return {"panel_signal": panel_signal, "panel_box": panel_box, "radiation": radiation, "reception": reception, "translation": translation, "list_source": list_source, "list_class": list_class, "list_count": list_count}


def aggregate_block(signal, owner, weights):
    count_rows = signal.shape[0]
    box_onehot = (owner[None, :] == jnp.arange(BOX_DEV, dtype=jnp.int32)[:, None]).astype(signal.dtype)
    masked = (signal[:, None, :] * box_onehot[None]).reshape(count_rows * BOX_DEV, PAN_DEV)
    summed = jnp.dot(masked, weights, preferred_element_type=jnp.float32)
    return summed.astype(jnp.bfloat16).reshape(count_rows, BOX_DEV, K)


def reference(panel_signal, panel_box, radiation, reception, translation, list_source, list_class, list_count):
    def outgoing_block(index):
        signal = lax.dynamic_slice_in_dim(panel_signal, index * PAN_DEV, PAN_DEV, 1)
        owner = lax.dynamic_slice_in_dim(panel_box, index * PAN_DEV, PAN_DEV, 0)
        weights = lax.dynamic_slice_in_dim(radiation, index * PAN_DEV, PAN_DEV, 0)
        return aggregate_block(signal, owner, weights)

    outgoing = lax.map(outgoing_block, jnp.arange(N_DOM, dtype=jnp.int32))
    outgoing = jnp.transpose(outgoing, (1, 0, 2, 3)).reshape(TS, B, K)
    used = (jnp.arange(J, dtype=jnp.int32)[None, :] < list_count[:, None])

    def direction_block(index):
        first = index * 32
        rays = lax.dynamic_slice_in_dim(outgoing, first, 32, 2)
        kernel = lax.dynamic_slice_in_dim(translation, first, 32, 2)
        lag_kernel = jnp.transpose(kernel, (1, 0, 2))[:, list_class, :] * used[None, :, :, None].astype(kernel.dtype)
        gathered = rays[:, list_source, :]
        result = []
        for step_out in range(TS):
            total = jnp.zeros((B, 32), jnp.float32)
            for step_in in range(step_out + 1):
                total = total + jnp.sum(lag_kernel[step_out - step_in].astype(jnp.float32) * gathered[step_in].astype(jnp.float32), axis=1)
            result.append(total.astype(jnp.bfloat16))
        return jnp.stack(result)

    incoming = lax.map(direction_block, jnp.arange(K // 32, dtype=jnp.int32))
    incoming = jnp.transpose(incoming, (1, 2, 0, 3)).reshape(TS, B, K)

    def field_block(index):
        rays = lax.dynamic_slice_in_dim(incoming, index * BOX_DEV, BOX_DEV, 1)
        owner = lax.dynamic_slice_in_dim(panel_box, index * PAN_DEV, PAN_DEV, 0)
        weights = lax.dynamic_slice_in_dim(reception, index * PAN_DEV, PAN_DEV, 0)
        partial_value = lax.dot_general(rays.reshape(TS * BOX_DEV, K), weights, (((1,), (1,)), ((), ())), preferred_element_type=jnp.float32)
        partial_value = partial_value.reshape(TS, BOX_DEV, PAN_DEV)
        box_onehot = (owner[None, :] == jnp.arange(BOX_DEV, dtype=jnp.int32)[:, None]).astype(jnp.float32)
        return jnp.sum(partial_value * box_onehot[None], axis=1).astype(jnp.bfloat16)

    field = lax.map(field_block, jnp.arange(N_DOM, dtype=jnp.int32))
    return jnp.transpose(field, (1, 0, 2)).reshape(TS, PAN)
```

```python
import jax
import jax.numpy as jnp
from jax import lax
from jax.experimental import pallas as pl
from jax.experimental.pallas import tpu as pltpu
from jax.sharding import PartitionSpec as P

BOX_DEV = 16
J = 8
N_DOM = 32
N_TM = 4
DIRS = 32
LAGS = 8
CLASSES = 64
BOXES = 512
PAN_DEV = 1024
K = 1024
GROUPS = K // 128
CHUNK = 128
N_CHUNK = BOXES // CHUNK
VMEM = pl.BlockSpec(memory_space=pltpu.VMEM)


def owner_rows(box_ref, half):
    row = lax.broadcasted_iota(jnp.int32, (8, PAN_DEV), 0) + 8 * half
    return box_ref[...] == row


def lane_group(shape):
    return lax.broadcasted_iota(jnp.int32, shape, len(shape) - 1) // DIRS


def aggregate_kernel(signal_ref, box_ref, radiation_ref, out_ref):
    signal = signal_ref[...].astype(jnp.float32)
    parts = []
    for half in range(2):
        mine = owner_rows(box_ref, half)
        for step in range(2):
            parts.append(jnp.where(mine, signal[step : step + 1, :], 0.0))
    masked = jnp.concatenate(parts, axis=0).astype(jnp.bfloat16)
    rays = jnp.dot(masked, radiation_ref[...], preferred_element_type=jnp.float32)
    group = lane_group((8, 128))
    for column in range(GROUPS):
        block = [rays[q * 8 : q * 8 + 8, column * 128 : column * 128 + 128] for q in range(4)]
        for g in range(4):
            tile = None
            for q in range(4):
                turn = ((q - g) % 4) * DIRS
                moved = block[q] if turn == 0 else pltpu.roll(block[q], turn, 1)
                tile = moved if tile is None else jnp.where(group == q, moved, tile)
            tile = tile.astype(jnp.bfloat16)
            for plane in range(N_TM):
                out_ref[(column * 4 + g) * N_TM + plane] = tile


def tables_kernel(source_ref, class_ref, count_ref, table_ref, pick_ref, weight_ref, rhs_ref):
    first = lax.axis_index("tm") * 2
    for step_out in range(2):
        for step_in in range(LAGS):
            lag = first + step_out - step_in
            start = pl.multiple_of(jnp.maximum(lag, 0) * DIRS, DIRS)
            rows = table_ref[pl.ds(start, DIRS), :]
            rows = jnp.where(lag >= 0, rows, jnp.zeros_like(rows))
            rhs_ref[pl.ds((step_out * LAGS + step_in) * DIRS, DIRS), :] = rows
    sources = source_ref[...]
    used = lax.broadcasted_iota(jnp.int32, (J, BOXES), 0) < count_ref[...]
    classes = jnp.where(used, class_ref[...], -1)
    sources = jnp.transpose(sources)
    classes = jnp.transpose(classes)
    lane_s = lax.broadcasted_iota(jnp.int32, (CHUNK, BOXES), 1)
    lane_c = lax.broadcasted_iota(jnp.int32, (CHUNK, CLASSES), 1)
    rhs = rhs_ref[...]
    for chunk in range(N_CHUNK):
        for j in range(J):
            rows = slice(chunk * CHUNK, chunk * CHUNK + CHUNK)
            at = pl.ds((chunk * J + j) * CHUNK, CHUNK)
            src = sources[rows, j : j + 1]
            cls = classes[rows, j : j + 1]
            pick_ref[at, :] = (src == lane_s).astype(jnp.float32).astype(jnp.bfloat16)
            hot = (cls == lane_c).astype(jnp.float32).astype(jnp.bfloat16)
            weight_ref[at, :] = lax.dot_general(
                hot, rhs, (((1,), (1,)), ((), ())), preferred_element_type=jnp.float32
            )


def translate_kernel(rays_ref, pick_ref, weight_ref, out_ref, near_ref, got_ref, sum_ref):
    low = lax.broadcasted_iota(jnp.int32, (N_DOM, 8, 128), 2) < 64
    for pair in range(2):
        left = rays_ref[:, 2 * pair].astype(jnp.float32)
        right = rays_ref[:, 2 * pair + 1].astype(jnp.float32)
        upper = jnp.where(low, left, pltpu.roll(right, 64, 2))
        lower = jnp.where(low, pltpu.roll(left, 64, 2), right)
        both = jnp.concatenate([upper[:, None], lower[:, None]], axis=1)
        near_ref[:, pair * 128 : pair * 128 + 128] = both.reshape(BOXES, 128).astype(jnp.bfloat16)
    rows_chunk = J * CHUNK
    for chunk in range(N_CHUNK):
        base = chunk * rows_chunk
        got_ref[...] = jnp.dot(
            pick_ref[base : base + rows_chunk, :],
            near_ref[...],
            preferred_element_type=jnp.float32,
        )
        for piece in range(CHUNK // 16):
            total = [jnp.zeros((16, 128), jnp.float32) for _ in range(2)]
            for j in range(J):
                at = j * CHUNK + piece * 16
                for side in range(2):
                    got = got_ref[at : at + 16, side * 128 : side * 128 + 128]
                    for step in range(2):
                        lanes = slice(step * 256 + side * 128, step * 256 + side * 128 + 128)
                        total[step] = total[step] + weight_ref[base + at : base + at + 16, lanes] * got
            for step in range(2):
                at = chunk * CHUNK + piece * 16
                sum_ref[at : at + 16, step * 128 : step * 128 + 128] = total[step]
    even = lane_group((N_DOM, 8, 128)) % 2 == 0
    merged = []
    for half in range(2):
        one = sum_ref[:, 0:128].reshape(N_DOM, 2, 8, 128)[:, half]
        two = sum_ref[:, 128:256].reshape(N_DOM, 2, 8, 128)[:, half]
        merged.append(
            jnp.where(even, one, two)
            + jnp.where(even, pltpu.roll(one, 96, 2), pltpu.roll(two, 32, 2))
        )
    final = jnp.where(low, merged[0], merged[1]) + pltpu.roll(
        jnp.where(low, merged[1], merged[0]), 64, 2
    )
    out_ref[...] = final.astype(jnp.bfloat16)


def receive_kernel(rays_ref, box_ref, reception_ref, out_ref):
    rays = rays_ref[...].astype(jnp.float32)
    turned = [rays] + [pltpu.roll(rays, DIRS * turn, 2) for turn in range(1, 4)]
    group = lane_group((8, 128))
    rows = []
    for q in range(4):
        columns = []
        for column in range(GROUPS):
            tile = None
            for g in range(4):
                moved = turned[(g - q) % 4][column * 4 + g]
                tile = moved if tile is None else jnp.where(group == g, moved, tile)
            columns.append(tile)
        rows.append(jnp.concatenate(columns, axis=1))
    incoming = jnp.concatenate(rows, axis=0).astype(jnp.bfloat16)
    field = lax.dot_general(
        incoming, reception_ref[...], (((1,), (1,)), ((), ())), preferred_element_type=jnp.float32
    )
    steps = []
    for step in range(2):
        total = jnp.zeros((1, PAN_DEV), jnp.float32)
        for half in range(2):
            q = half * 2 + step
            kept = jnp.where(owner_rows(box_ref, half), field[q * 8 : q * 8 + 8, :], 0.0)
            total = total + jnp.sum(kept, axis=0, keepdims=True)
        steps.append(total)
    out_ref[...] = jnp.concatenate(steps, axis=0).astype(jnp.bfloat16)


def params(mib):
    return pltpu.CompilerParams(vmem_limit_bytes=mib << 20)


def body(
    panel_signal, panel_box, radiation, reception, translation, list_source, list_class, list_count
):
    boxes_row = panel_box.reshape(1, PAN_DEV)
    blocks = pl.pallas_call(
        aggregate_kernel,
        out_shape=jax.ShapeDtypeStruct((N_DOM * N_TM, 8, 128), jnp.bfloat16),
        in_specs=[VMEM] * 3,
        out_specs=VMEM,
        compiler_params=params(16),
        name="aggregate",
    )(panel_signal, boxes_row, radiation)
    spread = lax.all_to_all(blocks, ("dom", "tm"), split_axis=0, concat_axis=0, tiled=True)

    pick, weight = pl.pallas_call(
        tables_kernel,
        out_shape=(
            jax.ShapeDtypeStruct((BOXES * J, BOXES), jnp.bfloat16),
            jax.ShapeDtypeStruct((BOXES * J, 2 * LAGS * DIRS), jnp.float32),
        ),
        in_specs=[VMEM] * 4,
        out_specs=(VMEM, VMEM),
        scratch_shapes=[pltpu.VMEM((2 * LAGS * DIRS, CLASSES), jnp.bfloat16)],
        compiler_params=params(32),
        cost_estimate=pl.CostEstimate(
            flops=2 * 4096 * 64 * 512, bytes_accessed=12 << 20, transcendentals=0
        ),
        name="tables",
    )(
        list_source.T,
        list_class.T,
        list_count.reshape(1, BOXES),
        jnp.transpose(translation, (1, 2, 0)).reshape(LAGS * DIRS, CLASSES),
    )

    incoming = pl.pallas_call(
        translate_kernel,
        out_shape=jax.ShapeDtypeStruct((N_DOM, 8, 128), jnp.bfloat16),
        in_specs=[VMEM] * 3,
        out_specs=VMEM,
        scratch_shapes=[
            pltpu.VMEM((BOXES, 256), jnp.bfloat16),
            pltpu.VMEM((J * CHUNK, 256), jnp.float32),
            pltpu.VMEM((BOXES, 256), jnp.float32),
        ],
        compiler_params=params(32),
        name="translate",
    )(spread.reshape(N_DOM, N_TM, 8, 128), pick, weight)

    rays = lax.all_to_all(incoming, "dom", split_axis=0, concat_axis=0, tiled=True)
    return pl.pallas_call(
        receive_kernel,
        out_shape=jax.ShapeDtypeStruct((2, PAN_DEV), jnp.bfloat16),
        in_specs=[VMEM] * 3,
        out_specs=VMEM,
        compiler_params=params(16),
        name="receive",
    )(rays, boxes_row, reception)


def solution(mesh):
    placed = (
        P("tm", "dom"),
        P("dom"),
        P("dom", None),
        P("dom", None),
        P(None, None, "dom"),
        P(),
        P(),
        P(),
    )
    return jax.shard_map(
        body, mesh=mesh, in_specs=placed, out_specs=P("tm", "dom"), check_vma=False
    )
```

```python
import jax
import jax.numpy as jnp
from jax import lax
from jax.experimental import pallas as pl
from jax.experimental.pallas import tpu as pltpu
from jax.sharding import PartitionSpec as P

BOX_DEV = 16
J = 8
N_DOM = 32
N_TM = 4
DIRS = 32
LAGS = 8
CLASSES = 64
BOXES = 512
PAN_DEV = 1024
K = 1024
GROUPS = K // 128
CHUNK = 128
N_CHUNK = BOXES // CHUNK
N_LOAD = 4
VMEM = pl.BlockSpec(memory_space=pltpu.VMEM)
HBM = pl.BlockSpec(memory_space=pltpu.HBM)


def owner_rows(box_ref, half):
    row = lax.broadcasted_iota(jnp.int32, (8, PAN_DEV), 0) + 8 * half
    return box_ref[...] == row


def lane_group(shape):
    return lax.broadcasted_iota(jnp.int32, shape, len(shape) - 1) // DIRS


def aggregate_kernel(
    signal_hbm, box_hbm, radiation_hbm, source_hbm, class_hbm, count_hbm,
    out_ref, pick_ref, hot_ref,
    signal_ref, box_ref, radiation_ref, source_ref, class_ref, count_ref, sems,
):
    small = [
        (source_hbm, source_ref),
        (class_hbm, class_ref),
        (count_hbm, count_ref),
        (signal_hbm, signal_ref),
        (box_hbm, box_ref),
    ]
    copies = [pltpu.make_async_copy(src, dst, sems.at[i]) for i, (src, dst) in enumerate(small)]
    height = PAN_DEV // N_LOAD
    for part in range(N_LOAD):
        rows = pl.ds(part * height, height)
        copies.append(
            pltpu.make_async_copy(
                radiation_hbm.at[rows], radiation_ref.at[rows], sems.at[len(small) + part]
            )
        )
    for copy in copies:
        copy.start()

    for copy in copies[:3]:
        copy.wait()
    used = lax.broadcasted_iota(jnp.int32, (J, BOXES), 0) < count_ref[...]
    classes = jnp.transpose(jnp.where(used, class_ref[...], -1))
    sources = jnp.transpose(source_ref[...])
    lane_s = lax.broadcasted_iota(jnp.int32, (CHUNK, BOXES), 1)
    lane_c = lax.broadcasted_iota(jnp.int32, (CHUNK, CLASSES), 1)
    for chunk in range(N_CHUNK):
        for j in range(J):
            rows = slice(chunk * CHUNK, chunk * CHUNK + CHUNK)
            at = pl.ds((chunk * J + j) * CHUNK, CHUNK)
            src = sources[rows, j : j + 1]
            cls = classes[rows, j : j + 1]
            pick_ref[at, :] = (src == lane_s).astype(jnp.float32).astype(jnp.bfloat16)
            hot_ref[at, :] = (cls == lane_c).astype(jnp.float32).astype(jnp.bfloat16)

    for copy in copies[3:5]:
        copy.wait()
    signal = signal_ref[...].astype(jnp.float32)
    parts = []
    for half in range(2):
        mine = owner_rows(box_ref, half)
        for step in range(2):
            parts.append(jnp.where(mine, signal[step : step + 1, :], 0.0))
    masked = jnp.concatenate(parts, axis=0).astype(jnp.bfloat16)
    rays = jnp.zeros((32, K), jnp.float32)
    for part in range(N_LOAD):
        copies[5 + part].wait()
        rows = slice(part * height, part * height + height)
        rays = rays + jnp.dot(
            masked[:, rows], radiation_ref[rows, :], preferred_element_type=jnp.float32
        )
    group = lane_group((8, 128))
    for column in range(GROUPS):
        block = [rays[q * 8 : q * 8 + 8, column * 128 : column * 128 + 128] for q in range(4)]
        for g in range(4):
            tile = None
            for q in range(4):
                turn = ((q - g) % 4) * DIRS
                moved = block[q] if turn == 0 else pltpu.roll(block[q], turn, 1)
                tile = moved if tile is None else jnp.where(group == q, moved, tile)
            tile = tile.astype(jnp.bfloat16)
            for plane in range(N_TM):
                out_ref[(column * 4 + g) * N_TM + plane] = tile


def translate_kernel(
    rays_ref, pick_ref, hot_ref, table_ref, out_ref, near_ref, rhs_ref, weight_ref, got_ref, sum_ref
):
    first = lax.axis_index("tm") * 2
    for step_out in range(2):
        for step_in in range(LAGS):
            lag = first + step_out - step_in
            start = pl.multiple_of(jnp.maximum(lag, 0) * DIRS, DIRS)
            rows = table_ref[pl.ds(start, DIRS), :]
            rows = jnp.where(lag >= 0, rows, jnp.zeros_like(rows))
            rhs_ref[pl.ds((step_out * LAGS + step_in) * DIRS, DIRS), :] = rows
    low = lax.broadcasted_iota(jnp.int32, (N_DOM, 8, 128), 2) < 64
    for pair in range(2):
        left = rays_ref[:, 2 * pair].astype(jnp.float32)
        right = rays_ref[:, 2 * pair + 1].astype(jnp.float32)
        upper = jnp.where(low, left, pltpu.roll(right, 64, 2))
        lower = jnp.where(low, pltpu.roll(left, 64, 2), right)
        both = jnp.concatenate([upper[:, None], lower[:, None]], axis=1)
        near_ref[:, pair * 128 : pair * 128 + 128] = both.reshape(BOXES, 128).astype(jnp.bfloat16)
    rows_chunk = J * CHUNK
    for chunk in range(N_CHUNK):
        base = chunk * rows_chunk
        rows = slice(base, base + rows_chunk)
        weight_ref[rows, :] = lax.dot_general(
            hot_ref[rows, :],
            rhs_ref[...],
            (((1,), (1,)), ((), ())),
            preferred_element_type=jnp.float32,
        )
        got_ref[rows, :] = jnp.dot(
            pick_ref[rows, :], near_ref[...], preferred_element_type=jnp.float32
        )
        for piece in range(CHUNK // 16):
            total = [jnp.zeros((16, 128), jnp.float32) for _ in range(2)]
            for j in range(J):
                at = base + j * CHUNK + piece * 16
                for side in range(2):
                    got = got_ref[at : at + 16, side * 128 : side * 128 + 128]
                    for step in range(2):
                        lanes = slice(step * 256 + side * 128, step * 256 + side * 128 + 128)
                        total[step] = total[step] + weight_ref[at : at + 16, lanes] * got
            for step in range(2):
                at = chunk * CHUNK + piece * 16
                sum_ref[at : at + 16, step * 128 : step * 128 + 128] = total[step]
    even = lane_group((N_DOM, 8, 128)) % 2 == 0
    merged = []
    for half in range(2):
        one = sum_ref[:, 0:128].reshape(N_DOM, 2, 8, 128)[:, half]
        two = sum_ref[:, 128:256].reshape(N_DOM, 2, 8, 128)[:, half]
        merged.append(
            jnp.where(even, one, two)
            + jnp.where(even, pltpu.roll(one, 96, 2), pltpu.roll(two, 32, 2))
        )
    final = jnp.where(low, merged[0], merged[1]) + pltpu.roll(
        jnp.where(low, merged[1], merged[0]), 64, 2
    )
    out_ref[...] = final.astype(jnp.bfloat16)


def receive_kernel(rays_ref, box_ref, reception_ref, out_ref):
    rays = rays_ref[...].astype(jnp.float32)
    turned = [rays] + [pltpu.roll(rays, DIRS * turn, 2) for turn in range(1, 4)]
    group = lane_group((8, 128))
    rows = []
    for q in range(4):
        columns = []
        for column in range(GROUPS):
            tile = None
            for g in range(4):
                moved = turned[(g - q) % 4][column * 4 + g]
                tile = moved if tile is None else jnp.where(group == g, moved, tile)
            columns.append(tile)
        rows.append(jnp.concatenate(columns, axis=1))
    incoming = jnp.concatenate(rows, axis=0).astype(jnp.bfloat16)
    field = lax.dot_general(
        incoming, reception_ref[...], (((1,), (1,)), ((), ())), preferred_element_type=jnp.float32
    )
    steps = []
    for step in range(2):
        total = jnp.zeros((1, PAN_DEV), jnp.float32)
        for half in range(2):
            q = half * 2 + step
            kept = jnp.where(owner_rows(box_ref, half), field[q * 8 : q * 8 + 8, :], 0.0)
            total = total + jnp.sum(kept, axis=0, keepdims=True)
        steps.append(total)
    out_ref[...] = jnp.concatenate(steps, axis=0).astype(jnp.bfloat16)


def in_hbm(array):
    return pltpu.with_memory_space_constraint(array, pltpu.HBM)


def params(mib):
    return pltpu.CompilerParams(vmem_limit_bytes=mib << 20)


def body(
    panel_signal, panel_box, radiation, reception, translation, list_source, list_class, list_count
):
    boxes_row = panel_box.reshape(1, PAN_DEV)
    blocks, pick, hot = pl.pallas_call(
        aggregate_kernel,
        out_shape=(
            jax.ShapeDtypeStruct((N_DOM * N_TM, 8, 128), jnp.bfloat16),
            jax.ShapeDtypeStruct((BOXES * J, BOXES), jnp.bfloat16),
            jax.ShapeDtypeStruct((BOXES * J, CLASSES), jnp.bfloat16),
        ),
        in_specs=[HBM] * 6,
        out_specs=(VMEM,) * 3,
        scratch_shapes=[
            pltpu.VMEM((2, PAN_DEV), jnp.bfloat16),
            pltpu.VMEM((1, PAN_DEV), jnp.int32),
            pltpu.VMEM((PAN_DEV, K), jnp.bfloat16),
            pltpu.VMEM((J, BOXES), jnp.int32),
            pltpu.VMEM((J, BOXES), jnp.int32),
            pltpu.VMEM((1, BOXES), jnp.int32),
            pltpu.SemaphoreType.DMA((5 + N_LOAD,)),
        ],
        compiler_params=params(40),
        name="aggregate",
    )(
        in_hbm(panel_signal),
        in_hbm(boxes_row),
        in_hbm(radiation),
        in_hbm(list_source.T),
        in_hbm(list_class.T),
        in_hbm(list_count.reshape(1, BOXES)),
    )
    spread = lax.all_to_all(blocks, ("dom", "tm"), split_axis=0, concat_axis=0, tiled=True)

    incoming = pl.pallas_call(
        translate_kernel,
        out_shape=jax.ShapeDtypeStruct((N_DOM, 8, 128), jnp.bfloat16),
        in_specs=[VMEM] * 4,
        out_specs=VMEM,
        scratch_shapes=[
            pltpu.VMEM((BOXES, 256), jnp.bfloat16),
            pltpu.VMEM((2 * LAGS * DIRS, CLASSES), jnp.bfloat16),
            pltpu.VMEM((BOXES * J, 512), jnp.float32),
            pltpu.VMEM((BOXES * J, 256), jnp.float32),
            pltpu.VMEM((BOXES, 256), jnp.float32),
        ],
        compiler_params=params(40),
        name="translate",
    )(
        spread.reshape(N_DOM, N_TM, 8, 128),
        pick,
        hot,
        jnp.transpose(translation, (1, 2, 0)).reshape(LAGS * DIRS, CLASSES),
    )

    rays = lax.all_to_all(incoming, "dom", split_axis=0, concat_axis=0, tiled=True)
    return pl.pallas_call(
        receive_kernel,
        out_shape=jax.ShapeDtypeStruct((2, PAN_DEV), jnp.bfloat16),
        in_specs=[VMEM] * 3,
        out_specs=VMEM,
        compiler_params=params(16),
        name="receive",
    )(rays, boxes_row, reception)


def solution(mesh):
    placed = (
        P("tm", "dom"),
        P("dom"),
        P("dom", None),
        P("dom", None),
        P(None, None, "dom"),
        P(),
        P(),
        P(),
    )
    return jax.shard_map(
        body, mesh=mesh, in_specs=placed, out_specs=P("tm", "dom"), check_vma=False
    )
```

```python
import jax
import jax.numpy as jnp
from jax import lax
from jax.experimental import pallas as pl
from jax.experimental.pallas import tpu as pltpu
from jax.sharding import PartitionSpec as P

BOX_DEV = 16
J = 8
N_DOM = 32
N_TM = 4
DIRS = 32
LAGS = 8
CLASSES = 64
BOXES = 512
PAN_DEV = 1024
K = 1024
GROUPS = K // 128
CHUNK = 128
N_CHUNK = BOXES // CHUNK
VMEM = pl.BlockSpec(memory_space=pltpu.VMEM)
HBM = pl.BlockSpec(memory_space=pltpu.HBM)


def owner_rows(box_ref, half):
    row = lax.broadcasted_iota(jnp.int32, (8, PAN_DEV), 0) + 8 * half
    return box_ref[...] == row


def lane_group(shape):
    return lax.broadcasted_iota(jnp.int32, shape, len(shape) - 1) // DIRS


def tables_kernel(
    source_hbm, class_hbm, count_hbm, table_hbm, signal_hbm, box_hbm, radiation_hbm,
    pick_ref, weight_ref, signal_ref, box_ref, radiation_ref,
    source_ref, class_ref, count_ref, table_ref, sems,
):
    pairs = [
        (source_hbm, source_ref),
        (class_hbm, class_ref),
        (count_hbm, count_ref),
        (table_hbm, table_ref),
        (signal_hbm, signal_ref),
        (box_hbm, box_ref),
        (radiation_hbm, radiation_ref),
    ]
    copies = [pltpu.make_async_copy(src, dst, sems.at[i]) for i, (src, dst) in enumerate(pairs)]
    for copy in copies:
        copy.start()
    for copy in copies[:4]:
        copy.wait()
    plane = lax.axis_index("tm")
    table = table_ref[...]
    blank = jnp.zeros((DIRS, CLASSES), jnp.bfloat16)
    parts = []
    for step_out in range(2):
        for back in range(N_TM):
            for step_in in range(2):
                lag = 2 * back + step_out - step_in
                if lag < 0:
                    parts.append(blank)
                    continue
                rows = table[lag * DIRS : lag * DIRS + DIRS, :]
                parts.append(jnp.where(plane >= back, rows, blank))
    rhs = jnp.concatenate(parts, axis=0)
    used = lax.broadcasted_iota(jnp.int32, (J, BOXES), 0) < count_ref[...]
    classes = jnp.transpose(jnp.where(used, class_ref[...], -1))
    sources = jnp.transpose(source_ref[...])
    lane_s = lax.broadcasted_iota(jnp.int32, (CHUNK, BOXES), 1)
    lane_c = lax.broadcasted_iota(jnp.int32, (CHUNK, CLASSES), 1)
    for chunk in range(N_CHUNK):
        for j in range(J):
            rows = slice(chunk * CHUNK, chunk * CHUNK + CHUNK)
            at = pl.ds((chunk * J + j) * CHUNK, CHUNK)
            src = sources[rows, j : j + 1]
            cls = classes[rows, j : j + 1]
            pick_ref[at, :] = (src == lane_s).astype(jnp.float32).astype(jnp.bfloat16)
            hot = (cls == lane_c).astype(jnp.float32).astype(jnp.bfloat16)
            weight_ref[at, :] = lax.dot_general(
                hot, rhs, (((1,), (1,)), ((), ())), preferred_element_type=jnp.float32
            )
    for copy in copies[4:]:
        copy.wait()


def aggregate_kernel(own_ref, one_ref, two_ref, three_ref, box_ref, radiation_ref, out_ref):
    mine = [owner_rows(box_ref, half) for half in range(2)]
    parts = []
    for ref in (own_ref, one_ref, two_ref, three_ref):
        signal = ref[...].astype(jnp.float32)
        for half in range(2):
            for step in range(2):
                parts.append(jnp.where(mine[half], signal[step : step + 1, :], 0.0))
    masked = jnp.concatenate(parts, axis=0).astype(jnp.bfloat16)
    rays = jnp.dot(masked, radiation_ref[...], preferred_element_type=jnp.float32)
    group = lane_group((8, 128))
    for back in range(N_TM):
        for column in range(GROUPS):
            lanes = slice(column * 128, column * 128 + 128)
            block = [rays[(back * 4 + q) * 8 : (back * 4 + q) * 8 + 8, lanes] for q in range(4)]
            for g in range(4):
                tile = None
                for q in range(4):
                    turn = ((q - g) % 4) * DIRS
                    moved = block[q] if turn == 0 else pltpu.roll(block[q], turn, 1)
                    tile = moved if tile is None else jnp.where(group == q, moved, tile)
                out_ref[(column * 4 + g) * N_TM + back] = tile.astype(jnp.bfloat16)


def translate_kernel(rays_ref, pick_ref, weight_ref, out_ref, near_ref, got_ref, sum_ref):
    low = lax.broadcasted_iota(jnp.int32, (N_DOM, 8, 128), 2) < 64
    for pair in range(2):
        left = rays_ref[:, 2 * pair].astype(jnp.float32)
        right = rays_ref[:, 2 * pair + 1].astype(jnp.float32)
        upper = jnp.where(low, left, pltpu.roll(right, 64, 2))
        lower = jnp.where(low, pltpu.roll(left, 64, 2), right)
        both = jnp.concatenate([upper[:, None], lower[:, None]], axis=1)
        near_ref[:, pair * 128 : pair * 128 + 128] = both.reshape(BOXES, 128).astype(jnp.bfloat16)
    rows_chunk = J * CHUNK
    for chunk in range(N_CHUNK):
        base = chunk * rows_chunk
        rows = slice(base, base + rows_chunk)
        got_ref[rows, :] = jnp.dot(
            pick_ref[rows, :], near_ref[...], preferred_element_type=jnp.float32
        )
        for piece in range(CHUNK // 16):
            total = [jnp.zeros((16, 128), jnp.float32) for _ in range(2)]
            for j in range(J):
                at = base + j * CHUNK + piece * 16
                for side in range(2):
                    got = got_ref[at : at + 16, side * 128 : side * 128 + 128]
                    for step in range(2):
                        lanes = slice(step * 256 + side * 128, step * 256 + side * 128 + 128)
                        total[step] = total[step] + weight_ref[at : at + 16, lanes] * got
            for step in range(2):
                at = chunk * CHUNK + piece * 16
                sum_ref[at : at + 16, step * 128 : step * 128 + 128] = total[step]
    even = lane_group((N_DOM, 8, 128)) % 2 == 0
    merged = []
    for half in range(2):
        one = sum_ref[:, 0:128].reshape(N_DOM, 2, 8, 128)[:, half]
        two = sum_ref[:, 128:256].reshape(N_DOM, 2, 8, 128)[:, half]
        merged.append(
            jnp.where(even, one, two)
            + jnp.where(even, pltpu.roll(one, 96, 2), pltpu.roll(two, 32, 2))
        )
    final = jnp.where(low, merged[0], merged[1]) + pltpu.roll(
        jnp.where(low, merged[1], merged[0]), 64, 2
    )
    out_ref[...] = final.astype(jnp.bfloat16)


def receive_kernel(rays_ref, box_ref, reception_ref, out_ref):
    rays = rays_ref[...].astype(jnp.float32)
    turned = [rays] + [pltpu.roll(rays, DIRS * turn, 2) for turn in range(1, 4)]
    group = lane_group((8, 128))
    rows = []
    for q in range(4):
        columns = []
        for column in range(GROUPS):
            tile = None
            for g in range(4):
                moved = turned[(g - q) % 4][column * 4 + g]
                tile = moved if tile is None else jnp.where(group == g, moved, tile)
            columns.append(tile)
        rows.append(jnp.concatenate(columns, axis=1))
    incoming = jnp.concatenate(rows, axis=0).astype(jnp.bfloat16)
    field = lax.dot_general(
        incoming, reception_ref[...], (((1,), (1,)), ((), ())), preferred_element_type=jnp.float32
    )
    steps = []
    for step in range(2):
        total = jnp.zeros((1, PAN_DEV), jnp.float32)
        for half in range(2):
            q = half * 2 + step
            kept = jnp.where(owner_rows(box_ref, half), field[q * 8 : q * 8 + 8, :], 0.0)
            total = total + jnp.sum(kept, axis=0, keepdims=True)
        steps.append(total)
    out_ref[...] = jnp.concatenate(steps, axis=0).astype(jnp.bfloat16)


def in_hbm(array):
    return pltpu.with_memory_space_constraint(array, pltpu.HBM)


def params(mib):
    return pltpu.CompilerParams(vmem_limit_bytes=mib << 20)


def body(
    panel_signal, panel_box, radiation, reception, translation, list_source, list_class, list_count
):
    boxes_row = panel_box.reshape(1, PAN_DEV)
    earlier = [
        lax.ppermute(panel_signal, "tm", [(p, (p + back) % N_TM) for p in range(N_TM)])
        for back in range(1, N_TM)
    ]
    pick, weight, own_signal, own_box, own_radiation = pl.pallas_call(
        tables_kernel,
        out_shape=(
            jax.ShapeDtypeStruct((BOXES * J, BOXES), jnp.bfloat16),
            jax.ShapeDtypeStruct((BOXES * J, 2 * LAGS * DIRS), jnp.float32),
            jax.ShapeDtypeStruct((2, PAN_DEV), jnp.bfloat16),
            jax.ShapeDtypeStruct((1, PAN_DEV), jnp.int32),
            jax.ShapeDtypeStruct((PAN_DEV, K), jnp.bfloat16),
        ),
        in_specs=[HBM] * 7,
        out_specs=(VMEM,) * 5,
        scratch_shapes=[
            pltpu.VMEM((J, BOXES), jnp.int32),
            pltpu.VMEM((J, BOXES), jnp.int32),
            pltpu.VMEM((1, BOXES), jnp.int32),
            pltpu.VMEM((LAGS * DIRS, CLASSES), jnp.bfloat16),
            pltpu.SemaphoreType.DMA((7,)),
        ],
        compiler_params=params(32),
        cost_estimate=pl.CostEstimate(
            flops=2 * 4096 * 64 * 512, bytes_accessed=12 << 20, transcendentals=0
        ),
        name="tables",
    )(
        in_hbm(list_source.T),
        in_hbm(list_class.T),
        in_hbm(list_count.reshape(1, BOXES)),
        in_hbm(jnp.transpose(translation, (1, 2, 0)).reshape(LAGS * DIRS, CLASSES)),
        in_hbm(panel_signal),
        in_hbm(boxes_row),
        in_hbm(radiation),
    )
    blocks = pl.pallas_call(
        aggregate_kernel,
        out_shape=jax.ShapeDtypeStruct((N_DOM * N_TM, 8, 128), jnp.bfloat16),
        in_specs=[VMEM] * 6,
        out_specs=VMEM,
        compiler_params=params(16),
        name="aggregate",
    )(own_signal, *earlier, own_box, own_radiation)
    spread = lax.all_to_all(blocks, "dom", split_axis=0, concat_axis=0, tiled=True)

    incoming = pl.pallas_call(
        translate_kernel,
        out_shape=jax.ShapeDtypeStruct((N_DOM, 8, 128), jnp.bfloat16),
        in_specs=[VMEM] * 3,
        out_specs=VMEM,
        scratch_shapes=[
            pltpu.VMEM((BOXES, 256), jnp.bfloat16),
            pltpu.VMEM((BOXES * J, 256), jnp.float32),
            pltpu.VMEM((BOXES, 256), jnp.float32),
        ],
        compiler_params=params(32),
        name="translate",
    )(spread.reshape(N_DOM, N_TM, 8, 128), pick, weight)

    rays = lax.all_to_all(incoming, "dom", split_axis=0, concat_axis=0, tiled=True)
    return pl.pallas_call(
        receive_kernel,
        out_shape=jax.ShapeDtypeStruct((2, PAN_DEV), jnp.bfloat16),
        in_specs=[VMEM] * 3,
        out_specs=VMEM,
        compiler_params=params(16),
        name="receive",
    )(rays, own_box, reception)


def solution(mesh):
    placed = (
        P("tm", "dom"),
        P("dom"),
        P("dom", None),
        P("dom", None),
        P(None, None, "dom"),
        P(),
        P(),
        P(),
    )
    return jax.shard_map(
        body, mesh=mesh, in_specs=placed, out_specs=P("tm", "dom"), check_vma=False
    )
```

```python
import jax
import jax.numpy as jnp
from jax import lax
from jax.experimental import pallas as pl
from jax.experimental.pallas import tpu as pltpu
from jax.sharding import PartitionSpec as P

BOX_DEV = 16
J = 8
N_DOM = 32
N_TM = 4
DIRS = 32
LAGS = 8
CLASSES = 64
BOXES = 512
PAN_DEV = 1024
K = 1024
GROUPS = K // 128
CHUNK = 128
N_CHUNK = BOXES // CHUNK
N_LOAD = 4
VMEM = pl.BlockSpec(memory_space=pltpu.VMEM)
HBM = pl.BlockSpec(memory_space=pltpu.HBM)


def owner_rows(box_ref, half):
    row = lax.broadcasted_iota(jnp.int32, (8, PAN_DEV), 0) + 8 * half
    return box_ref[...] == row


def lane_group(shape):
    return lax.broadcasted_iota(jnp.int32, shape, len(shape) - 1) // DIRS


def aggregate_kernel(
    signal_hbm, box_hbm, radiation_hbm, source_hbm, class_hbm, count_hbm, table_hbm,
    out_ref, pick_ref, weight_ref, box_ref,
    signal_ref, radiation_ref, source_ref, class_ref, count_ref, table_ref, rhs_ref, sems,
):
    small = [
        (source_hbm, source_ref),
        (class_hbm, class_ref),
        (count_hbm, count_ref),
        (table_hbm, table_ref),
        (signal_hbm, signal_ref),
        (box_hbm, box_ref),
    ]
    copies = [pltpu.make_async_copy(src, dst, sems.at[i]) for i, (src, dst) in enumerate(small)]
    height = PAN_DEV // N_LOAD
    for part in range(N_LOAD):
        rows = pl.ds(part * height, height)
        copies.append(
            pltpu.make_async_copy(
                radiation_hbm.at[rows], radiation_ref.at[rows], sems.at[len(small) + part]
            )
        )
    for copy in copies:
        copy.start()

    for copy in copies[:4]:
        copy.wait()
    first = lax.axis_index("tm") * 2
    for step_out in range(2):
        for step_in in range(LAGS):
            lag = first + step_out - step_in
            start = pl.multiple_of(jnp.maximum(lag, 0) * DIRS, DIRS)
            rows = table_ref[pl.ds(start, DIRS), :]
            rows = jnp.where(lag >= 0, rows, jnp.zeros_like(rows))
            rhs_ref[pl.ds((step_out * LAGS + step_in) * DIRS, DIRS), :] = rows
    rhs = rhs_ref[...]
    used = lax.broadcasted_iota(jnp.int32, (J, BOXES), 0) < count_ref[...]
    classes = jnp.transpose(jnp.where(used, class_ref[...], -1))
    sources = jnp.transpose(source_ref[...])
    lane_s = lax.broadcasted_iota(jnp.int32, (CHUNK, BOXES), 1)
    lane_c = lax.broadcasted_iota(jnp.int32, (CHUNK, CLASSES), 1)
    for chunk in range(N_CHUNK):
        hots = []
        for j in range(J):
            rows = slice(chunk * CHUNK, chunk * CHUNK + CHUNK)
            at = pl.ds((chunk * J + j) * CHUNK, CHUNK)
            src = sources[rows, j : j + 1]
            cls = classes[rows, j : j + 1]
            pick_ref[at, :] = (src == lane_s).astype(jnp.float32).astype(jnp.bfloat16)
            hots.append((cls == lane_c).astype(jnp.float32).astype(jnp.bfloat16))
        weight_ref[pl.ds(chunk * J * CHUNK, J * CHUNK), :] = lax.dot_general(
            jnp.concatenate(hots, axis=0),
            rhs,
            (((1,), (1,)), ((), ())),
            preferred_element_type=jnp.float32,
        )

    for copy in copies[4:6]:
        copy.wait()
    signal = signal_ref[...].astype(jnp.float32)
    parts = []
    for half in range(2):
        mine = owner_rows(box_ref, half)
        for step in range(2):
            parts.append(jnp.where(mine, signal[step : step + 1, :], 0.0))
    masked = jnp.concatenate(parts, axis=0).astype(jnp.bfloat16)
    rays = jnp.zeros((32, K), jnp.float32)
    for part in range(N_LOAD):
        copies[6 + part].wait()
        rows = slice(part * height, part * height + height)
        rays = rays + jnp.dot(
            masked[:, rows], radiation_ref[rows, :], preferred_element_type=jnp.float32
        )
    group = lane_group((8, 128))
    for column in range(GROUPS):
        block = [rays[q * 8 : q * 8 + 8, column * 128 : column * 128 + 128] for q in range(4)]
        for g in range(4):
            tile = None
            for q in range(4):
                turn = ((q - g) % 4) * DIRS
                moved = block[q] if turn == 0 else pltpu.roll(block[q], turn, 1)
                tile = moved if tile is None else jnp.where(group == q, moved, tile)
            tile = tile.astype(jnp.bfloat16)
            for plane in range(N_TM):
                out_ref[(column * 4 + g) * N_TM + plane] = tile


def translate_kernel(rays_ref, pick_ref, weight_ref, out_ref, near_ref, got_ref, sum_ref):
    low = lax.broadcasted_iota(jnp.int32, (N_DOM, 8, 128), 2) < 64
    for pair in range(2):
        left = rays_ref[:, 2 * pair].astype(jnp.float32)
        right = rays_ref[:, 2 * pair + 1].astype(jnp.float32)
        upper = jnp.where(low, left, pltpu.roll(right, 64, 2))
        lower = jnp.where(low, pltpu.roll(left, 64, 2), right)
        both = jnp.concatenate([upper[:, None], lower[:, None]], axis=1)
        near_ref[:, pair * 128 : pair * 128 + 128] = both.reshape(BOXES, 128).astype(jnp.bfloat16)
    rows_chunk = J * CHUNK
    for chunk in range(N_CHUNK):
        base = chunk * rows_chunk
        rows = slice(base, base + rows_chunk)
        got_ref[rows, :] = jnp.dot(
            pick_ref[rows, :], near_ref[...], preferred_element_type=jnp.float32
        )
        for piece in range(CHUNK // 16):
            total = [jnp.zeros((16, 128), jnp.float32) for _ in range(2)]
            for j in range(J):
                at = base + j * CHUNK + piece * 16
                for side in range(2):
                    got = got_ref[at : at + 16, side * 128 : side * 128 + 128]
                    for step in range(2):
                        lanes = slice(step * 256 + side * 128, step * 256 + side * 128 + 128)
                        total[step] = total[step] + weight_ref[at : at + 16, lanes] * got
            for step in range(2):
                at = chunk * CHUNK + piece * 16
                sum_ref[at : at + 16, step * 128 : step * 128 + 128] = total[step]
    even = lane_group((N_DOM, 8, 128)) % 2 == 0
    merged = []
    for half in range(2):
        one = sum_ref[:, 0:128].reshape(N_DOM, 2, 8, 128)[:, half]
        two = sum_ref[:, 128:256].reshape(N_DOM, 2, 8, 128)[:, half]
        merged.append(
            jnp.where(even, one, two)
            + jnp.where(even, pltpu.roll(one, 96, 2), pltpu.roll(two, 32, 2))
        )
    final = jnp.where(low, merged[0], merged[1]) + pltpu.roll(
        jnp.where(low, merged[1], merged[0]), 64, 2
    )
    out_ref[...] = final.astype(jnp.bfloat16)


def receive_kernel(rays_ref, box_ref, reception_ref, out_ref):
    rays = rays_ref[...].astype(jnp.float32)
    turned = [rays] + [pltpu.roll(rays, DIRS * turn, 2) for turn in range(1, 4)]
    group = lane_group((8, 128))
    rows = []
    for q in range(4):
        columns = []
        for column in range(GROUPS):
            tile = None
            for g in range(4):
                moved = turned[(g - q) % 4][column * 4 + g]
                tile = moved if tile is None else jnp.where(group == g, moved, tile)
            columns.append(tile)
        rows.append(jnp.concatenate(columns, axis=1))
    incoming = jnp.concatenate(rows, axis=0).astype(jnp.bfloat16)
    field = lax.dot_general(
        incoming, reception_ref[...], (((1,), (1,)), ((), ())), preferred_element_type=jnp.float32
    )
    steps = []
    for step in range(2):
        total = jnp.zeros((1, PAN_DEV), jnp.float32)
        for half in range(2):
            q = half * 2 + step
            kept = jnp.where(owner_rows(box_ref, half), field[q * 8 : q * 8 + 8, :], 0.0)
            total = total + jnp.sum(kept, axis=0, keepdims=True)
        steps.append(total)
    out_ref[...] = jnp.concatenate(steps, axis=0).astype(jnp.bfloat16)


def in_hbm(array):
    return pltpu.with_memory_space_constraint(array, pltpu.HBM)


def params(mib):
    return pltpu.CompilerParams(vmem_limit_bytes=mib << 20)


def body(
    panel_signal, panel_box, radiation, reception, translation, list_source, list_class, list_count
):
    boxes_row = panel_box.reshape(1, PAN_DEV)
    blocks, pick, weight, own_box = pl.pallas_call(
        aggregate_kernel,
        out_shape=(
            jax.ShapeDtypeStruct((N_DOM * N_TM, 8, 128), jnp.bfloat16),
            jax.ShapeDtypeStruct((BOXES * J, BOXES), jnp.bfloat16),
            jax.ShapeDtypeStruct((BOXES * J, 2 * LAGS * DIRS), jnp.float32),
            jax.ShapeDtypeStruct((1, PAN_DEV), jnp.int32),
        ),
        in_specs=[HBM] * 7,
        out_specs=(VMEM,) * 4,
        scratch_shapes=[
            pltpu.VMEM((2, PAN_DEV), jnp.bfloat16),
            pltpu.VMEM((PAN_DEV, K), jnp.bfloat16),
            pltpu.VMEM((J, BOXES), jnp.int32),
            pltpu.VMEM((J, BOXES), jnp.int32),
            pltpu.VMEM((1, BOXES), jnp.int32),
            pltpu.VMEM((LAGS * DIRS, CLASSES), jnp.bfloat16),
            pltpu.VMEM((2 * LAGS * DIRS, CLASSES), jnp.bfloat16),
            pltpu.SemaphoreType.DMA((6 + N_LOAD,)),
        ],
        compiler_params=params(40),
        name="aggregate",
    )(
        in_hbm(panel_signal),
        in_hbm(boxes_row),
        in_hbm(radiation),
        in_hbm(list_source.T),
        in_hbm(list_class.T),
        in_hbm(list_count.reshape(1, BOXES)),
        in_hbm(jnp.transpose(translation, (1, 2, 0)).reshape(LAGS * DIRS, CLASSES)),
    )
    spread = lax.all_to_all(blocks, ("dom", "tm"), split_axis=0, concat_axis=0, tiled=True)

    incoming = pl.pallas_call(
        translate_kernel,
        out_shape=jax.ShapeDtypeStruct((N_DOM, 8, 128), jnp.bfloat16),
        in_specs=[VMEM] * 3,
        out_specs=VMEM,
        scratch_shapes=[
            pltpu.VMEM((BOXES, 256), jnp.bfloat16),
            pltpu.VMEM((BOXES * J, 256), jnp.float32),
            pltpu.VMEM((BOXES, 256), jnp.float32),
        ],
        compiler_params=params(32),
        name="translate",
    )(spread.reshape(N_DOM, N_TM, 8, 128), pick, weight)

    rays = lax.all_to_all(incoming, "dom", split_axis=0, concat_axis=0, tiled=True)
    return pl.pallas_call(
        receive_kernel,
        out_shape=jax.ShapeDtypeStruct((2, PAN_DEV), jnp.bfloat16),
        in_specs=[VMEM] * 3,
        out_specs=VMEM,
        compiler_params=params(16),
        name="receive",
    )(rays, own_box, reception)


def solution(mesh):
    placed = (
        P("tm", "dom"),
        P("dom"),
        P("dom", None),
        P("dom", None),
        P(None, None, "dom"),
        P(),
        P(),
        P(),
    )
    return jax.shard_map(
        body, mesh=mesh, in_specs=placed, out_specs=P("tm", "dom"), check_vma=False
    )
```

```python
import jax
import jax.numpy as jnp
from jax import lax
from jax.experimental import pallas as pl
from jax.experimental.pallas import tpu as pltpu
from jax.sharding import PartitionSpec as P

BOX_DEV = 16
J = 8
N_DOM = 32
N_TM = 4
DIRS = 32
LAGS = 8
CLASSES = 64
BOXES = 512
PAN_DEV = 1024
K = 1024
GROUPS = K // 128
N_CHUNK = BOXES // 128
N_LOAD = 8
VMEM = pl.BlockSpec(memory_space=pltpu.VMEM)
HBM = pl.BlockSpec(memory_space=pltpu.HBM)


def owner_rows(box_ref, half):
    row = lax.broadcasted_iota(jnp.int32, (8, PAN_DEV), 0) + 8 * half
    return box_ref[...] == row


def lane_group(shape):
    return lax.broadcasted_iota(jnp.int32, shape, len(shape) - 1) // DIRS


def aggregate_kernel(
    signal_hbm, box_hbm, radiation_hbm, source_hbm, class_hbm, count_hbm, table_hbm,
    out_ref, pick_ref, weight_ref, box_ref,
    signal_ref, radiation_ref, source_ref, class_ref, count_ref, table_ref, sems,
):
    small = [
        (source_hbm, source_ref),
        (class_hbm, class_ref),
        (count_hbm, count_ref),
        (table_hbm, table_ref),
        (signal_hbm, signal_ref),
        (box_hbm, box_ref),
    ]
    copies = [pltpu.make_async_copy(src, dst, sems.at[i]) for i, (src, dst) in enumerate(small)]
    height = PAN_DEV // N_LOAD
    for part in range(N_LOAD):
        rows = pl.ds(part * height, height)
        copies.append(
            pltpu.make_async_copy(
                radiation_hbm.at[rows], radiation_ref.at[rows], sems.at[len(small) + part]
            )
        )
    for copy in copies:
        copy.start()

    row = lax.broadcasted_iota(jnp.int32, (16, 128), 0)
    pattern = row // 8 * BOX_DEV + row % 8
    kind = lax.broadcasted_iota(jnp.int32, (CLASSES, 128), 0)
    one, zero = jnp.bfloat16(1), jnp.bfloat16(0)
    for copy in copies[:4]:
        copy.wait()
    first = lax.axis_index("tm") * 2
    parts = []
    for step in range(LAGS):
        lag = first + 1 - step
        start = pl.multiple_of(jnp.maximum(lag, 0) * DIRS, DIRS)
        rows = table_ref[pl.ds(start, DIRS), :]
        parts.append(jnp.where(lag >= 0, rows, jnp.zeros_like(rows)))
    lagged = jnp.concatenate(parts, axis=0)
    used = lax.broadcasted_iota(jnp.int32, (J, BOXES), 0) < count_ref[...]
    classes = jnp.where(used, class_ref[...], -1)
    sources = source_ref[...]
    wide = [
        jnp.broadcast_to(sources[j : j + 1, at : at + 128], (16, 128)).astype(jnp.int16)
        for at in range(0, BOXES, 128)
        for j in range(J)
    ]
    for chunk in range(N_CHUNK):
        lanes = slice(chunk * 128, chunk * 128 + 128)
        hots = [
            (classes[j : j + 1, lanes] == kind).astype(jnp.float32).astype(jnp.bfloat16)
            for j in range(J)
        ]
        at = slice(chunk * J * 128, (chunk + 1) * J * 128)
        weight_ref[:, at] = jnp.dot(
            lagged, jnp.concatenate(hots, axis=1), preferred_element_type=jnp.float32
        )
        for low in range(chunk * 128, chunk * 128 + 128, 16):
            box = low % 256 // 8 * BOX_DEV + low // 256 * 8
            here = (pattern + box).astype(jnp.int16)
            for index, source in enumerate(wide):
                pick_ref[low : low + 16, index * 128 : index * 128 + 128] = jnp.where(
                    source == here, one, zero
                )

    for copy in copies[4:6]:
        copy.wait()
    signal = signal_ref[...].astype(jnp.float32)
    parts = []
    for half in range(2):
        mine = owner_rows(box_ref, half)
        for step in range(2):
            parts.append(jnp.where(mine, signal[step : step + 1, :], 0.0))
    masked = jnp.concatenate(parts, axis=0).astype(jnp.bfloat16)
    rays = jnp.zeros((32, K), jnp.float32)
    for part in range(N_LOAD):
        copies[6 + part].wait()
        rows = slice(part * height, part * height + height)
        rays = rays + jnp.dot(
            masked[:, rows], radiation_ref[rows, :], preferred_element_type=jnp.float32
        )
    group = lane_group((8, 128))
    for column in range(GROUPS):
        block = [rays[q * 8 : q * 8 + 8, column * 128 : column * 128 + 128] for q in range(4)]
        for g in range(4):
            tile = None
            for q in range(4):
                turn = ((q - g) % 4) * DIRS
                moved = block[q] if turn == 0 else pltpu.roll(block[q], turn, 1)
                tile = moved if tile is None else jnp.where(group == q, moved, tile)
            tile = tile.astype(jnp.bfloat16)
            for plane in range(N_TM):
                out_ref[(column * 4 + g) * N_TM + plane] = tile


def translate_kernel(rays_ref, pick_ref, weight_ref, out_ref, near_ref, got_ref, sum_ref):
    for plane in range(N_TM):
        turned = jnp.transpose(rays_ref[:, plane].astype(jnp.float32).reshape(256, 128))
        turned = turned.astype(jnp.bfloat16)
        for half in range(2):
            near_ref[plane * 64 : plane * 64 + 64, half * 256 : half * 256 + 256] = turned[
                half * 64 : half * 64 + 64
            ]
    for chunk in range(N_CHUNK):
        at = slice(chunk * J * 128, (chunk + 1) * J * 128)
        got_ref[:, at] = jnp.dot(
            near_ref[...], pick_ref[:, at], preferred_element_type=jnp.float32
        )
        for low in range(0, DIRS, 8):
            total = [jnp.zeros((8, 128), jnp.float32) for _ in range(2)]
            for j in range(J):
                lanes = slice((chunk * J + j) * 128, (chunk * J + j) * 128 + 128)
                for step in range(LAGS):
                    weight = weight_ref[step * DIRS + low : step * DIRS + low + 8, lanes]
                    at_step = step * DIRS + low
                    total[1] = total[1] + weight * got_ref[at_step : at_step + 8, lanes]
                    if step > 0:
                        at_step = at_step - DIRS
                        total[0] = total[0] + weight * got_ref[at_step : at_step + 8, lanes]
            for step in range(2):
                at_row = chunk % 2 * 64 + step * DIRS + low
                sum_ref[at_row : at_row + 8, chunk // 2 * 128 : chunk // 2 * 128 + 128] = total[
                    step
                ]
        if chunk % 2 == 1:
            pair = jnp.transpose(sum_ref[:, chunk // 2 * 128 : chunk // 2 * 128 + 128])
            pair = pair.reshape(8, 2, 8, 128)
            upper, lower = pair[:, 0], pair[:, 1]
            left = lax.broadcasted_iota(jnp.int32, (8, 8, 128), 2) < 64
            tiles = (
                jnp.where(left, upper, pltpu.roll(lower, 64, 2)),
                jnp.where(left, pltpu.roll(upper, 64, 2), lower),
            )
            for side in range(2):
                at_box = (chunk - 1 + side) * 8
                out_ref[at_box : at_box + 8] = tiles[side].astype(jnp.bfloat16)


def receive_kernel(rays_ref, box_ref, reception_ref, out_ref):
    rays = rays_ref[...].astype(jnp.float32)
    turned = [rays] + [pltpu.roll(rays, DIRS * turn, 2) for turn in range(1, 4)]
    group = lane_group((8, 128))
    rows = []
    for q in range(4):
        columns = []
        for column in range(GROUPS):
            tile = None
            for g in range(4):
                moved = turned[(g - q) % 4][column * 4 + g]
                tile = moved if tile is None else jnp.where(group == g, moved, tile)
            columns.append(tile)
        rows.append(jnp.concatenate(columns, axis=1))
    incoming = jnp.concatenate(rows, axis=0).astype(jnp.bfloat16)
    field = lax.dot_general(
        incoming, reception_ref[...], (((1,), (1,)), ((), ())), preferred_element_type=jnp.float32
    )
    steps = []
    for step in range(2):
        total = jnp.zeros((1, PAN_DEV), jnp.float32)
        for half in range(2):
            q = half * 2 + step
            kept = jnp.where(owner_rows(box_ref, half), field[q * 8 : q * 8 + 8, :], 0.0)
            total = total + jnp.sum(kept, axis=0, keepdims=True)
        steps.append(total)
    out_ref[...] = jnp.concatenate(steps, axis=0).astype(jnp.bfloat16)


def in_hbm(array):
    return pltpu.with_memory_space_constraint(array, pltpu.HBM)


def params(mib):
    return pltpu.CompilerParams(vmem_limit_bytes=mib << 20)


def body(
    panel_signal, panel_box, radiation, reception, translation, list_source, list_class, list_count
):
    boxes_row = panel_box.reshape(1, PAN_DEV)
    blocks, pick, weight, own_box = pl.pallas_call(
        aggregate_kernel,
        out_shape=(
            jax.ShapeDtypeStruct((N_DOM * N_TM, 8, 128), jnp.bfloat16),
            jax.ShapeDtypeStruct((BOXES, BOXES * J), jnp.bfloat16),
            jax.ShapeDtypeStruct((LAGS * DIRS, BOXES * J), jnp.float32),
            jax.ShapeDtypeStruct((1, PAN_DEV), jnp.int32),
        ),
        in_specs=[HBM] * 7,
        out_specs=(VMEM,) * 4,
        scratch_shapes=[
            pltpu.VMEM((2, PAN_DEV), jnp.bfloat16),
            pltpu.VMEM((PAN_DEV, K), jnp.bfloat16),
            pltpu.VMEM((J, BOXES), jnp.int32),
            pltpu.VMEM((J, BOXES), jnp.int32),
            pltpu.VMEM((1, BOXES), jnp.int32),
            pltpu.VMEM((LAGS * DIRS, CLASSES), jnp.bfloat16),
            pltpu.SemaphoreType.DMA((6 + N_LOAD,)),
        ],
        compiler_params=params(40),
        name="aggregate",
    )(
        in_hbm(panel_signal),
        in_hbm(boxes_row),
        in_hbm(radiation),
        in_hbm(list_source.T),
        in_hbm(list_class.T),
        in_hbm(list_count.reshape(1, BOXES)),
        in_hbm(jnp.transpose(translation, (1, 2, 0)).reshape(LAGS * DIRS, CLASSES)),
    )
    spread = lax.all_to_all(blocks, ("dom", "tm"), split_axis=0, concat_axis=0, tiled=True)

    incoming = pl.pallas_call(
        translate_kernel,
        out_shape=jax.ShapeDtypeStruct((N_DOM, 8, 128), jnp.bfloat16),
        in_specs=[VMEM] * 3,
        out_specs=VMEM,
        scratch_shapes=[
            pltpu.VMEM((LAGS * DIRS, BOXES), jnp.bfloat16),
            pltpu.VMEM((LAGS * DIRS, BOXES * J), jnp.float32),
            pltpu.VMEM((128, BOXES // 2), jnp.float32),
        ],
        compiler_params=params(32),
        name="translate",
    )(spread.reshape(N_DOM, N_TM, 8, 128), pick, weight)

    rays = lax.all_to_all(incoming, "dom", split_axis=0, concat_axis=0, tiled=True)
    return pl.pallas_call(
        receive_kernel,
        out_shape=jax.ShapeDtypeStruct((2, PAN_DEV), jnp.bfloat16),
        in_specs=[VMEM] * 3,
        out_specs=VMEM,
        compiler_params=params(16),
        name="receive",
    )(rays, own_box, reception)


def solution(mesh):
    placed = (
        P("tm", "dom"),
        P("dom"),
        P("dom", None),
        P("dom", None),
        P(None, None, "dom"),
        P(),
        P(),
        P(),
    )
    return jax.shard_map(
        body, mesh=mesh, in_specs=placed, out_specs=P("tm", "dom"), check_vma=False
    )
```

```python
import jax
import jax.numpy as jnp
from jax import lax
from jax.experimental import pallas as pl
from jax.experimental.pallas import tpu as pltpu
from jax.sharding import PartitionSpec as P

BOX_DEV = 16
J = 8
N_DOM = 32
N_TM = 4
DIRS = 32
LAGS = 8
CLASSES = 64
BOXES = 512
PAN_DEV = 1024
K = 1024
GROUPS = K // 128
N_CHUNK = BOXES // 128
N_LOAD = 1
VMEM = pl.BlockSpec(memory_space=pltpu.VMEM)
HBM = pl.BlockSpec(memory_space=pltpu.HBM)


def owner_rows(box_ref, half):
    row = lax.broadcasted_iota(jnp.int32, (8, PAN_DEV), 0) + 8 * half
    return box_ref[...] == row


def lane_group(shape):
    return lax.broadcasted_iota(jnp.int32, shape, len(shape) - 1) // DIRS


def aggregate_kernel(
    signal_hbm, box_hbm, radiation_hbm, source_hbm, class_hbm, count_hbm, table_hbm,
    out_ref, pick_ref, weight_ref, box_ref,
    signal_ref, radiation_ref, source_ref, class_ref, count_ref, table_ref, sems,
):
    small = [
        (source_hbm, source_ref),
        (class_hbm, class_ref),
        (count_hbm, count_ref),
        (table_hbm, table_ref),
        (signal_hbm, signal_ref),
        (box_hbm, box_ref),
    ]
    copies = [pltpu.make_async_copy(src, dst, sems.at[i]) for i, (src, dst) in enumerate(small)]
    height = PAN_DEV // N_LOAD
    for part in range(N_LOAD):
        rows = pl.ds(part * height, height)
        copies.append(
            pltpu.make_async_copy(
                radiation_hbm.at[rows], radiation_ref.at[rows], sems.at[len(small) + part]
            )
        )
    for copy in copies:
        copy.start()

    row = lax.broadcasted_iota(jnp.int32, (16, 128), 0)
    pattern = row // 8 * BOX_DEV + row % 8
    kind = lax.broadcasted_iota(jnp.int32, (CLASSES, 128), 0)
    one, zero = jnp.bfloat16(1), jnp.bfloat16(0)
    for copy in copies[:4]:
        copy.wait()
    first = lax.axis_index("tm") * 2
    parts = []
    for step in range(LAGS):
        lag = first + 1 - step
        start = pl.multiple_of(jnp.maximum(lag, 0) * DIRS, DIRS)
        rows = table_ref[pl.ds(start, DIRS), :]
        parts.append(jnp.where(lag >= 0, rows, jnp.zeros_like(rows)))
    lagged = jnp.concatenate(parts, axis=0)
    used = lax.broadcasted_iota(jnp.int32, (J, BOXES), 0) < count_ref[...]
    classes = jnp.where(used, class_ref[...], -1)
    sources = source_ref[...]
    wide = [
        jnp.broadcast_to(sources[j : j + 1, at : at + 128], (16, 128)).astype(jnp.int16)
        for at in range(0, BOXES, 128)
        for j in range(J)
    ]
    for chunk in range(N_CHUNK):
        lanes = slice(chunk * 128, chunk * 128 + 128)
        hots = [
            (classes[j : j + 1, lanes] == kind).astype(jnp.float32).astype(jnp.bfloat16)
            for j in range(J)
        ]
        at = slice(chunk * J * 128, (chunk + 1) * J * 128)
        weight_ref[:, at] = jnp.dot(
            lagged, jnp.concatenate(hots, axis=1), preferred_element_type=jnp.float32
        )
        for low in range(chunk * 128, chunk * 128 + 128, 16):
            box = low % 256 // 8 * BOX_DEV + low // 256 * 8
            here = (pattern + box).astype(jnp.int16)
            for index, source in enumerate(wide):
                pick_ref[low : low + 16, index * 128 : index * 128 + 128] = jnp.where(
                    source == here, one, zero
                )

    for copy in copies[4:6]:
        copy.wait()
    signal = signal_ref[...].astype(jnp.float32)
    parts = []
    for half in range(2):
        mine = owner_rows(box_ref, half)
        for step in range(2):
            parts.append(jnp.where(mine, signal[step : step + 1, :], 0.0))
    masked = jnp.concatenate(parts, axis=0).astype(jnp.bfloat16)
    rays = jnp.zeros((32, K), jnp.float32)
    for part in range(N_LOAD):
        copies[6 + part].wait()
        rows = slice(part * height, part * height + height)
        rays = rays + jnp.dot(
            masked[:, rows], radiation_ref[rows, :], preferred_element_type=jnp.float32
        )
    group = lane_group((8, 128))
    for column in range(GROUPS):
        block = [rays[q * 8 : q * 8 + 8, column * 128 : column * 128 + 128] for q in range(4)]
        for g in range(4):
            tile = None
            for q in range(4):
                turn = ((q - g) % 4) * DIRS
                moved = block[q] if turn == 0 else pltpu.roll(block[q], turn, 1)
                tile = moved if tile is None else jnp.where(group == q, moved, tile)
            tile = tile.astype(jnp.bfloat16)
            for plane in range(N_TM):
                out_ref[(column * 4 + g) * N_TM + plane] = tile


def translate_kernel(rays_ref, pick_ref, weight_ref, out_ref, near_ref, got_ref, sum_ref):
    for plane in range(N_TM):
        turned = jnp.transpose(rays_ref[:, plane].astype(jnp.float32).reshape(256, 128))
        turned = turned.astype(jnp.bfloat16)
        for half in range(2):
            near_ref[plane * 64 : plane * 64 + 64, half * 256 : half * 256 + 256] = turned[
                half * 64 : half * 64 + 64
            ]
    for chunk in range(N_CHUNK):
        at = slice(chunk * J * 128, (chunk + 1) * J * 128)
        got_ref[:, at] = jnp.dot(
            near_ref[...], pick_ref[:, at], preferred_element_type=jnp.float32
        )
        total = [jnp.zeros((DIRS, 128), jnp.float32) for _ in range(2)]
        for j in range(J):
            lanes = slice((chunk * J + j) * 128, (chunk * J + j) * 128 + 128)
            weight, got = weight_ref[0:DIRS, lanes], got_ref[0:DIRS, lanes]
            even, odd = None, weight * got
            for step in range(1, LAGS):
                here = slice(step * DIRS, step * DIRS + DIRS)
                weight = weight_ref[here, lanes]
                even = weight * got if even is None else even + weight * got
                got = got_ref[here, lanes]
                odd = odd + weight * got
            total = [total[0] + even, total[1] + odd]
        for step in range(2):
            at_row = chunk % 2 * 64 + step * DIRS
            sum_ref[at_row : at_row + DIRS, chunk // 2 * 128 : chunk // 2 * 128 + 128] = total[step]
        if chunk % 2 == 1:
            pair = jnp.transpose(sum_ref[:, chunk // 2 * 128 : chunk // 2 * 128 + 128])
            pair = pair.reshape(8, 2, 8, 128)
            upper, lower = pair[:, 0], pair[:, 1]
            left = lax.broadcasted_iota(jnp.int32, (8, 8, 128), 2) < 64
            tiles = (
                jnp.where(left, upper, pltpu.roll(lower, 64, 2)),
                jnp.where(left, pltpu.roll(upper, 64, 2), lower),
            )
            for side in range(2):
                at_box = (chunk - 1 + side) * 8
                out_ref[at_box : at_box + 8] = tiles[side].astype(jnp.bfloat16)


def receive_kernel(rays_ref, box_ref, reception_ref, out_ref):
    rays = rays_ref[...].astype(jnp.float32)
    turned = [rays] + [pltpu.roll(rays, DIRS * turn, 2) for turn in range(1, 4)]
    group = lane_group((8, 128))
    rows = []
    for q in range(4):
        columns = []
        for column in range(GROUPS):
            tile = None
            for g in range(4):
                moved = turned[(g - q) % 4][column * 4 + g]
                tile = moved if tile is None else jnp.where(group == g, moved, tile)
            columns.append(tile)
        rows.append(jnp.concatenate(columns, axis=1))
    incoming = jnp.concatenate(rows, axis=0).astype(jnp.bfloat16)
    field = lax.dot_general(
        incoming, reception_ref[...], (((1,), (1,)), ((), ())), preferred_element_type=jnp.float32
    )
    steps = []
    for step in range(2):
        total = jnp.zeros((1, PAN_DEV), jnp.float32)
        for half in range(2):
            q = half * 2 + step
            kept = jnp.where(owner_rows(box_ref, half), field[q * 8 : q * 8 + 8, :], 0.0)
            total = total + jnp.sum(kept, axis=0, keepdims=True)
        steps.append(total)
    out_ref[...] = jnp.concatenate(steps, axis=0).astype(jnp.bfloat16)


def in_hbm(array):
    return pltpu.with_memory_space_constraint(array, pltpu.HBM)


def params(mib):
    return pltpu.CompilerParams(vmem_limit_bytes=mib << 20)


def body(
    panel_signal, panel_box, radiation, reception, translation, list_source, list_class, list_count
):
    boxes_row = panel_box.reshape(1, PAN_DEV)
    blocks, pick, weight, own_box = pl.pallas_call(
        aggregate_kernel,
        out_shape=(
            jax.ShapeDtypeStruct((N_DOM * N_TM, 8, 128), jnp.bfloat16),
            jax.ShapeDtypeStruct((BOXES, BOXES * J), jnp.bfloat16),
            jax.ShapeDtypeStruct((LAGS * DIRS, BOXES * J), jnp.float32),
            jax.ShapeDtypeStruct((1, PAN_DEV), jnp.int32),
        ),
        in_specs=[HBM] * 7,
        out_specs=(VMEM,) * 4,
        scratch_shapes=[
            pltpu.VMEM((2, PAN_DEV), jnp.bfloat16),
            pltpu.VMEM((PAN_DEV, K), jnp.bfloat16),
            pltpu.VMEM((J, BOXES), jnp.int32),
            pltpu.VMEM((J, BOXES), jnp.int32),
            pltpu.VMEM((1, BOXES), jnp.int32),
            pltpu.VMEM((LAGS * DIRS, CLASSES), jnp.bfloat16),
            pltpu.SemaphoreType.DMA((6 + N_LOAD,)),
        ],
        compiler_params=params(40),
        name="aggregate",
    )(
        in_hbm(panel_signal),
        in_hbm(boxes_row),
        in_hbm(radiation),
        in_hbm(list_source.T),
        in_hbm(list_class.T),
        in_hbm(list_count.reshape(1, BOXES)),
        in_hbm(jnp.transpose(translation, (1, 2, 0)).reshape(LAGS * DIRS, CLASSES)),
    )
    spread = lax.all_to_all(blocks, ("dom", "tm"), split_axis=0, concat_axis=0, tiled=True)

    incoming = pl.pallas_call(
        translate_kernel,
        out_shape=jax.ShapeDtypeStruct((N_DOM, 8, 128), jnp.bfloat16),
        in_specs=[VMEM] * 3,
        out_specs=VMEM,
        scratch_shapes=[
            pltpu.VMEM((LAGS * DIRS, BOXES), jnp.bfloat16),
            pltpu.VMEM((LAGS * DIRS, BOXES * J), jnp.float32),
            pltpu.VMEM((128, BOXES // 2), jnp.float32),
        ],
        compiler_params=params(32),
        name="translate",
    )(spread.reshape(N_DOM, N_TM, 8, 128), pick, weight)

    rays = lax.all_to_all(incoming, "dom", split_axis=0, concat_axis=0, tiled=True)
    return pl.pallas_call(
        receive_kernel,
        out_shape=jax.ShapeDtypeStruct((2, PAN_DEV), jnp.bfloat16),
        in_specs=[VMEM] * 3,
        out_specs=VMEM,
        compiler_params=params(16),
        name="receive",
    )(rays, own_box, reception)


def solution(mesh):
    placed = (
        P("tm", "dom"),
        P("dom"),
        P("dom", None),
        P("dom", None),
        P(None, None, "dom"),
        P(),
        P(),
        P(),
    )
    return jax.shard_map(
        body, mesh=mesh, in_specs=placed, out_specs=P("tm", "dom"), check_vma=False
    )
```

```python
import jax
import jax.numpy as jnp
from jax import lax
from jax.experimental import pallas as pl
from jax.experimental.pallas import tpu as pltpu
from jax.sharding import PartitionSpec as P

BOX_DEV = 16
J = 8
N_DOM = 32
N_TM = 4
DIRS = 32
LAGS = 8
CLASSES = 64
BOXES = 512
PAN_DEV = 1024
K = 1024
GROUPS = K // 128
N_CHUNK = BOXES // 128
N_LOAD = 1
VMEM = pl.BlockSpec(memory_space=pltpu.VMEM)
HBM = pl.BlockSpec(memory_space=pltpu.HBM)


def owner_rows(box_ref, half):
    row = lax.broadcasted_iota(jnp.int32, (8, PAN_DEV), 0) + 8 * half
    return box_ref[...] == row


def lane_group(shape):
    return lax.broadcasted_iota(jnp.int32, shape, len(shape) - 1) // DIRS


def aggregate_kernel(
    signal_hbm, box_hbm, radiation_hbm, source_hbm, class_hbm, count_hbm, table_hbm,
    out_ref, pick_ref, weight_ref, box_ref,
    signal_ref, radiation_ref, source_ref, class_ref, count_ref, table_ref, sems,
):
    small = [
        (source_hbm, source_ref),
        (class_hbm, class_ref),
        (count_hbm, count_ref),
        (table_hbm, table_ref),
        (signal_hbm, signal_ref),
        (box_hbm, box_ref),
    ]
    copies = [pltpu.make_async_copy(src, dst, sems.at[i]) for i, (src, dst) in enumerate(small)]
    height = PAN_DEV // N_LOAD
    for part in range(N_LOAD):
        rows = pl.ds(part * height, height)
        copies.append(
            pltpu.make_async_copy(
                radiation_hbm.at[rows], radiation_ref.at[rows], sems.at[len(small) + part]
            )
        )
    for copy in copies:
        copy.start()

    row = lax.broadcasted_iota(jnp.int32, (16, 128), 0)
    pattern = row // 8 * BOX_DEV + row % 8
    kind = lax.broadcasted_iota(jnp.int32, (CLASSES, 128), 0)
    one, zero = jnp.bfloat16(1), jnp.bfloat16(0)
    for copy in copies[:4]:
        copy.wait()
    first = lax.axis_index("tm") * 2
    parts = []
    for step in range(LAGS):
        lag = first + 1 - step
        start = pl.multiple_of(jnp.maximum(lag, 0) * DIRS, DIRS)
        rows = table_ref[pl.ds(start, DIRS), :]
        parts.append(jnp.where(lag >= 0, rows, jnp.zeros_like(rows)))
    lagged = jnp.concatenate(parts, axis=0)
    used = lax.broadcasted_iota(jnp.int32, (J, BOXES), 0) < count_ref[...]
    classes = jnp.where(used, class_ref[...], -1)
    sources = source_ref[...]
    wide = [
        jnp.broadcast_to(sources[j : j + 1, at : at + 128], (16, 128)).astype(jnp.int16)
        for at in range(0, BOXES, 128)
        for j in range(J)
    ]
    for low in range(0, BOXES, 16):
        box = low % 256 // 8 * BOX_DEV + low // 256 * 8
        here = (pattern + box).astype(jnp.int16)
        for index, source in enumerate(wide):
            pick_ref[low : low + 16, index * 128 : index * 128 + 128] = jnp.where(
                source == here, one, zero
            )
    for chunk in range(N_CHUNK):
        lanes = slice(chunk * 128, chunk * 128 + 128)
        hots = [
            (classes[j : j + 1, lanes] == kind).astype(jnp.float32).astype(jnp.bfloat16)
            for j in range(J)
        ]
        at = slice(chunk * J * 128, (chunk + 1) * J * 128)
        weight_ref[:, at] = jnp.dot(
            lagged, jnp.concatenate(hots, axis=1), preferred_element_type=jnp.float32
        )

    for copy in copies[4:6]:
        copy.wait()
    signal = signal_ref[...].astype(jnp.float32)
    parts = []
    for half in range(2):
        mine = owner_rows(box_ref, half)
        for step in range(2):
            parts.append(jnp.where(mine, signal[step : step + 1, :], 0.0))
    masked = jnp.concatenate(parts, axis=0).astype(jnp.bfloat16)
    rays = jnp.zeros((32, K), jnp.float32)
    for part in range(N_LOAD):
        copies[6 + part].wait()
        rows = slice(part * height, part * height + height)
        rays = rays + jnp.dot(
            masked[:, rows], radiation_ref[rows, :], preferred_element_type=jnp.float32
        )
    group = lane_group((8, 128))
    for column in range(GROUPS):
        block = [rays[q * 8 : q * 8 + 8, column * 128 : column * 128 + 128] for q in range(4)]
        for g in range(4):
            tile = None
            for q in range(4):
                turn = ((q - g) % 4) * DIRS
                moved = block[q] if turn == 0 else pltpu.roll(block[q], turn, 1)
                tile = moved if tile is None else jnp.where(group == q, moved, tile)
            tile = tile.astype(jnp.bfloat16)
            for plane in range(N_TM):
                out_ref[(column * 4 + g) * N_TM + plane] = tile


def translate_kernel(rays_ref, pick_ref, weight_ref, out_ref, near_ref, got_ref, sum_ref):
    for plane in range(N_TM):
        turned = jnp.transpose(rays_ref[:, plane].reshape(256, 128))
        for half in range(2):
            near_ref[plane * 64 : plane * 64 + 64, half * 256 : half * 256 + 256] = turned[
                half * 64 : half * 64 + 64
            ]
    for chunk in range(N_CHUNK):
        at = slice(chunk * J * 128, (chunk + 1) * J * 128)
        got_ref[:, at] = jnp.dot(
            near_ref[...], pick_ref[:, at], preferred_element_type=jnp.float32
        )
        total = [jnp.zeros((DIRS, 128), jnp.float32) for _ in range(2)]
        for j in range(J):
            lanes = slice((chunk * J + j) * 128, (chunk * J + j) * 128 + 128)
            weight, got = weight_ref[0:DIRS, lanes], got_ref[0:DIRS, lanes]
            even, odd = None, weight * got
            for step in range(1, LAGS):
                here = slice(step * DIRS, step * DIRS + DIRS)
                weight = weight_ref[here, lanes]
                even = weight * got if even is None else even + weight * got
                got = got_ref[here, lanes]
                odd = odd + weight * got
            total = [total[0] + even, total[1] + odd]
        for step in range(2):
            at_row = chunk % 2 * 64 + step * DIRS
            sum_ref[at_row : at_row + DIRS, chunk // 2 * 128 : chunk // 2 * 128 + 128] = total[step]
        if chunk % 2 == 1:
            pair = jnp.transpose(sum_ref[:, chunk // 2 * 128 : chunk // 2 * 128 + 128])
            pair = pair.reshape(8, 2, 8, 128)
            upper, lower = pair[:, 0], pair[:, 1]
            left = lax.broadcasted_iota(jnp.int32, (8, 8, 128), 2) < 64
            tiles = (
                jnp.where(left, upper, pltpu.roll(lower, 64, 2)),
                jnp.where(left, pltpu.roll(upper, 64, 2), lower),
            )
            for side in range(2):
                at_box = (chunk - 1 + side) * 8
                out_ref[at_box : at_box + 8] = tiles[side].astype(jnp.bfloat16)


def receive_kernel(rays_ref, box_ref, reception_ref, out_ref):
    rays = rays_ref[...].astype(jnp.float32)
    turned = [rays] + [pltpu.roll(rays, DIRS * turn, 2) for turn in range(1, 4)]
    group = lane_group((8, 128))
    rows = []
    for q in range(4):
        columns = []
        for column in range(GROUPS):
            tile = None
            for g in range(4):
                moved = turned[(g - q) % 4][column * 4 + g]
                tile = moved if tile is None else jnp.where(group == g, moved, tile)
            columns.append(tile)
        rows.append(jnp.concatenate(columns, axis=1))
    incoming = jnp.concatenate(rows, axis=0).astype(jnp.bfloat16)
    field = lax.dot_general(
        incoming, reception_ref[...], (((1,), (1,)), ((), ())), preferred_element_type=jnp.float32
    )
    steps = []
    for step in range(2):
        total = jnp.zeros((1, PAN_DEV), jnp.float32)
        for half in range(2):
            q = half * 2 + step
            kept = jnp.where(owner_rows(box_ref, half), field[q * 8 : q * 8 + 8, :], 0.0)
            total = total + jnp.sum(kept, axis=0, keepdims=True)
        steps.append(total)
    out_ref[...] = jnp.concatenate(steps, axis=0).astype(jnp.bfloat16)


def in_hbm(array):
    return pltpu.with_memory_space_constraint(array, pltpu.HBM)


def params(mib):
    return pltpu.CompilerParams(vmem_limit_bytes=mib << 20)


def body(
    panel_signal, panel_box, radiation, reception, translation, list_source, list_class, list_count
):
    boxes_row = panel_box.reshape(1, PAN_DEV)
    blocks, pick, weight, own_box = pl.pallas_call(
        aggregate_kernel,
        out_shape=(
            jax.ShapeDtypeStruct((N_DOM * N_TM, 8, 128), jnp.bfloat16),
            jax.ShapeDtypeStruct((BOXES, BOXES * J), jnp.bfloat16),
            jax.ShapeDtypeStruct((LAGS * DIRS, BOXES * J), jnp.float32),
            jax.ShapeDtypeStruct((1, PAN_DEV), jnp.int32),
        ),
        in_specs=[HBM] * 7,
        out_specs=(VMEM,) * 4,
        scratch_shapes=[
            pltpu.VMEM((2, PAN_DEV), jnp.bfloat16),
            pltpu.VMEM((PAN_DEV, K), jnp.bfloat16),
            pltpu.VMEM((J, BOXES), jnp.int32),
            pltpu.VMEM((J, BOXES), jnp.int32),
            pltpu.VMEM((1, BOXES), jnp.int32),
            pltpu.VMEM((LAGS * DIRS, CLASSES), jnp.bfloat16),
            pltpu.SemaphoreType.DMA((6 + N_LOAD,)),
        ],
        compiler_params=params(40),
        name="aggregate",
    )(
        in_hbm(panel_signal),
        in_hbm(boxes_row),
        in_hbm(radiation),
        in_hbm(list_source.T),
        in_hbm(list_class.T),
        in_hbm(list_count.reshape(1, BOXES)),
        in_hbm(jnp.transpose(translation, (1, 2, 0)).reshape(LAGS * DIRS, CLASSES)),
    )
    spread = lax.all_to_all(blocks, ("dom", "tm"), split_axis=0, concat_axis=0, tiled=True)

    incoming = pl.pallas_call(
        translate_kernel,
        out_shape=jax.ShapeDtypeStruct((N_DOM, 8, 128), jnp.bfloat16),
        in_specs=[VMEM] * 3,
        out_specs=VMEM,
        scratch_shapes=[
            pltpu.VMEM((LAGS * DIRS, BOXES), jnp.bfloat16),
            pltpu.VMEM((LAGS * DIRS, BOXES * J), jnp.float32),
            pltpu.VMEM((128, BOXES // 2), jnp.float32),
        ],
        compiler_params=params(32),
        name="translate",
    )(spread.reshape(N_DOM, N_TM, 8, 128), pick, weight)

    rays = lax.all_to_all(incoming, "dom", split_axis=0, concat_axis=0, tiled=True)
    return pl.pallas_call(
        receive_kernel,
        out_shape=jax.ShapeDtypeStruct((2, PAN_DEV), jnp.bfloat16),
        in_specs=[VMEM] * 3,
        out_specs=VMEM,
        compiler_params=params(16),
        name="receive",
    )(rays, own_box, reception)


def solution(mesh):
    placed = (
        P("tm", "dom"),
        P("dom"),
        P("dom", None),
        P("dom", None),
        P(None, None, "dom"),
        P(),
        P(),
        P(),
    )
    return jax.shard_map(
        body, mesh=mesh, in_specs=placed, out_specs=P("tm", "dom"), check_vma=False
    )
```

```python
import jax
import jax.numpy as jnp
from jax import lax
from jax.experimental import pallas as pl
from jax.experimental.pallas import tpu as pltpu
from jax.sharding import PartitionSpec as P

BOX_DEV = 16
J = 8
N_DOM = 32
N_TM = 4
DIRS = 32
LAGS = 8
CLASSES = 64
BOXES = 512
PAN_DEV = 1024
K = 1024
GROUPS = K // 128
N_CHUNK = BOXES // 128
N_LOAD = 1
VMEM = pl.BlockSpec(memory_space=pltpu.VMEM)
HBM = pl.BlockSpec(memory_space=pltpu.HBM)


def owner_rows(box_ref, half):
    row = lax.broadcasted_iota(jnp.int32, (8, PAN_DEV), 0) + 8 * half
    return box_ref[...] == row


def lane_group(shape):
    return lax.broadcasted_iota(jnp.int32, shape, len(shape) - 1) // DIRS


def aggregate_kernel(
    signal_hbm, box_hbm, radiation_hbm, source_hbm, class_hbm, count_hbm, table_hbm,
    out_ref, pick_ref, weight_ref, box_ref,
    signal_ref, radiation_ref, source_ref, class_ref, count_ref, table_ref, sems,
):
    small = [
        (source_hbm, source_ref),
        (class_hbm, class_ref),
        (count_hbm, count_ref),
        (table_hbm, table_ref),
        (signal_hbm, signal_ref),
        (box_hbm, box_ref),
    ]
    copies = [pltpu.make_async_copy(src, dst, sems.at[i]) for i, (src, dst) in enumerate(small)]
    height = PAN_DEV // N_LOAD
    for part in range(N_LOAD):
        rows = pl.ds(part * height, height)
        copies.append(
            pltpu.make_async_copy(
                radiation_hbm.at[rows], radiation_ref.at[rows], sems.at[len(small) + part]
            )
        )
    for copy in copies:
        copy.start()

    row = lax.broadcasted_iota(jnp.int32, (16, 128), 0)
    pattern = row // 8 * BOX_DEV + row % 8
    kind = lax.broadcasted_iota(jnp.int32, (CLASSES, 128), 0).astype(jnp.int16)
    one, zero = jnp.bfloat16(1), jnp.bfloat16(0)
    for copy in copies[:4]:
        copy.wait()
    first = lax.axis_index("tm") * 2
    parts = []
    for step in range(LAGS):
        lag = first + 1 - step
        start = pl.multiple_of(jnp.maximum(lag, 0) * DIRS, DIRS)
        rows = table_ref[pl.ds(start, DIRS), :]
        parts.append(jnp.where(lag >= 0, rows, jnp.zeros_like(rows)))
    lagged = jnp.concatenate(parts, axis=0)
    used = lax.broadcasted_iota(jnp.int32, (J, BOXES), 0) < count_ref[...]
    classes = jnp.where(used, class_ref[...], -1)
    sources = source_ref[...]
    wide = [
        jnp.broadcast_to(sources[j : j + 1, at : at + 128], (16, 128)).astype(jnp.int16)
        for at in range(0, BOXES, 128)
        for j in range(J)
    ]
    for low in range(0, BOXES, 16):
        box = low % 256 // 8 * BOX_DEV + low // 256 * 8
        here = (pattern + box).astype(jnp.int16)
        for index, source in enumerate(wide):
            pick_ref[low : low + 16, index * 128 : index * 128 + 128] = jnp.where(
                source == here, one, zero
            )
    for chunk in range(N_CHUNK):
        lanes = slice(chunk * 128, chunk * 128 + 128)
        hots = []
        for j in range(J):
            wanted = jnp.broadcast_to(classes[j : j + 1, lanes], (16, 128)).astype(jnp.int16)
            parts = [
                jnp.where(wanted == kind[low : low + 16], one, zero)
                for low in range(0, CLASSES, 16)
            ]
            hots.append(jnp.concatenate(parts, axis=0))
        at = slice(chunk * J * 128, (chunk + 1) * J * 128)
        weight_ref[:, at] = jnp.dot(
            lagged, jnp.concatenate(hots, axis=1), preferred_element_type=jnp.float32
        )

    for copy in copies[4:6]:
        copy.wait()
    signal = signal_ref[...].astype(jnp.float32)
    parts = []
    for half in range(2):
        mine = owner_rows(box_ref, half)
        for step in range(2):
            parts.append(jnp.where(mine, signal[step : step + 1, :], 0.0))
    masked = jnp.concatenate(parts, axis=0).astype(jnp.bfloat16)
    rays = jnp.zeros((32, K), jnp.float32)
    for part in range(N_LOAD):
        copies[6 + part].wait()
        rows = slice(part * height, part * height + height)
        rays = rays + jnp.dot(
            masked[:, rows], radiation_ref[rows, :], preferred_element_type=jnp.float32
        )
    group = lane_group((8, 128))
    for column in range(GROUPS):
        block = [rays[q * 8 : q * 8 + 8, column * 128 : column * 128 + 128] for q in range(4)]
        for g in range(4):
            tile = None
            for q in range(4):
                turn = ((q - g) % 4) * DIRS
                moved = block[q] if turn == 0 else pltpu.roll(block[q], turn, 1)
                tile = moved if tile is None else jnp.where(group == q, moved, tile)
            tile = tile.astype(jnp.bfloat16)
            for plane in range(N_TM):
                out_ref[(column * 4 + g) * N_TM + plane] = tile


def translate_kernel(rays_ref, pick_ref, weight_ref, out_ref, near_ref, got_ref, sum_ref):
    for plane in range(N_TM):
        turned = jnp.transpose(rays_ref[:, plane].reshape(256, 128))
        for half in range(2):
            near_ref[plane * 64 : plane * 64 + 64, half * 256 : half * 256 + 256] = turned[
                half * 64 : half * 64 + 64
            ]
    for chunk in range(N_CHUNK):
        at = slice(chunk * J * 128, (chunk + 1) * J * 128)
        got_ref[:, at] = jnp.dot(
            near_ref[...], pick_ref[:, at], preferred_element_type=jnp.float32
        )
        total = [jnp.zeros((DIRS, 128), jnp.float32) for _ in range(2)]
        for j in range(J):
            lanes = slice((chunk * J + j) * 128, (chunk * J + j) * 128 + 128)
            weight, got = weight_ref[0:DIRS, lanes], got_ref[0:DIRS, lanes]
            even, odd = None, weight * got
            for step in range(1, LAGS):
                here = slice(step * DIRS, step * DIRS + DIRS)
                weight = weight_ref[here, lanes]
                even = weight * got if even is None else even + weight * got
                got = got_ref[here, lanes]
                odd = odd + weight * got
            total = [total[0] + even, total[1] + odd]
        for step in range(2):
            at_row = chunk % 2 * 64 + step * DIRS
            sum_ref[at_row : at_row + DIRS, chunk // 2 * 128 : chunk // 2 * 128 + 128] = total[step]
        if chunk % 2 == 1:
            pair = jnp.transpose(sum_ref[:, chunk // 2 * 128 : chunk // 2 * 128 + 128])
            pair = pair.reshape(8, 2, 8, 128)
            upper, lower = pair[:, 0], pair[:, 1]
            left = lax.broadcasted_iota(jnp.int32, (8, 8, 128), 2) < 64
            tiles = (
                jnp.where(left, upper, pltpu.roll(lower, 64, 2)),
                jnp.where(left, pltpu.roll(upper, 64, 2), lower),
            )
            for side in range(2):
                at_box = (chunk - 1 + side) * 8
                out_ref[at_box : at_box + 8] = tiles[side].astype(jnp.bfloat16)


def receive_kernel(rays_ref, box_ref, reception_ref, out_ref):
    rays = rays_ref[...].astype(jnp.float32)
    turned = [rays] + [pltpu.roll(rays, DIRS * turn, 2) for turn in range(1, 4)]
    group = lane_group((8, 128))
    rows = []
    for q in range(4):
        columns = []
        for column in range(GROUPS):
            tile = None
            for g in range(4):
                moved = turned[(g - q) % 4][column * 4 + g]
                tile = moved if tile is None else jnp.where(group == g, moved, tile)
            columns.append(tile)
        rows.append(jnp.concatenate(columns, axis=1))
    incoming = jnp.concatenate(rows, axis=0).astype(jnp.bfloat16)
    field = lax.dot_general(
        incoming, reception_ref[...], (((1,), (1,)), ((), ())), preferred_element_type=jnp.float32
    )
    steps = []
    for step in range(2):
        total = jnp.zeros((1, PAN_DEV), jnp.float32)
        for half in range(2):
            q = half * 2 + step
            kept = jnp.where(owner_rows(box_ref, half), field[q * 8 : q * 8 + 8, :], 0.0)
            total = total + jnp.sum(kept, axis=0, keepdims=True)
        steps.append(total)
    out_ref[...] = jnp.concatenate(steps, axis=0).astype(jnp.bfloat16)


def in_hbm(array):
    return pltpu.with_memory_space_constraint(array, pltpu.HBM)


def params(mib):
    return pltpu.CompilerParams(vmem_limit_bytes=mib << 20)


def body(
    panel_signal, panel_box, radiation, reception, translation, list_source, list_class, list_count
):
    boxes_row = panel_box.reshape(1, PAN_DEV)
    blocks, pick, weight, own_box = pl.pallas_call(
        aggregate_kernel,
        out_shape=(
            jax.ShapeDtypeStruct((N_DOM * N_TM, 8, 128), jnp.bfloat16),
            jax.ShapeDtypeStruct((BOXES, BOXES * J), jnp.bfloat16),
            jax.ShapeDtypeStruct((LAGS * DIRS, BOXES * J), jnp.float32),
            jax.ShapeDtypeStruct((1, PAN_DEV), jnp.int32),
        ),
        in_specs=[HBM] * 7,
        out_specs=(VMEM,) * 4,
        scratch_shapes=[
            pltpu.VMEM((2, PAN_DEV), jnp.bfloat16),
            pltpu.VMEM((PAN_DEV, K), jnp.bfloat16),
            pltpu.VMEM((J, BOXES), jnp.int32),
            pltpu.VMEM((J, BOXES), jnp.int32),
            pltpu.VMEM((1, BOXES), jnp.int32),
            pltpu.VMEM((LAGS * DIRS, CLASSES), jnp.bfloat16),
            pltpu.SemaphoreType.DMA((6 + N_LOAD,)),
        ],
        compiler_params=params(40),
        name="aggregate",
    )(
        in_hbm(panel_signal),
        in_hbm(boxes_row),
        in_hbm(radiation),
        in_hbm(list_source.T),
        in_hbm(list_class.T),
        in_hbm(list_count.reshape(1, BOXES)),
        in_hbm(jnp.transpose(translation, (1, 2, 0)).reshape(LAGS * DIRS, CLASSES)),
    )
    spread = lax.all_to_all(blocks, ("dom", "tm"), split_axis=0, concat_axis=0, tiled=True)

    incoming = pl.pallas_call(
        translate_kernel,
        out_shape=jax.ShapeDtypeStruct((N_DOM, 8, 128), jnp.bfloat16),
        in_specs=[VMEM] * 3,
        out_specs=VMEM,
        scratch_shapes=[
            pltpu.VMEM((LAGS * DIRS, BOXES), jnp.bfloat16),
            pltpu.VMEM((LAGS * DIRS, BOXES * J), jnp.float32),
            pltpu.VMEM((128, BOXES // 2), jnp.float32),
        ],
        compiler_params=params(32),
        name="translate",
    )(spread.reshape(N_DOM, N_TM, 8, 128), pick, weight)

    rays = lax.all_to_all(incoming, "dom", split_axis=0, concat_axis=0, tiled=True)
    return pl.pallas_call(
        receive_kernel,
        out_shape=jax.ShapeDtypeStruct((2, PAN_DEV), jnp.bfloat16),
        in_specs=[VMEM] * 3,
        out_specs=VMEM,
        compiler_params=params(16),
        name="receive",
    )(rays, own_box, reception)


def solution(mesh):
    placed = (
        P("tm", "dom"),
        P("dom"),
        P("dom", None),
        P("dom", None),
        P(None, None, "dom"),
        P(),
        P(),
        P(),
    )
    return jax.shard_map(
        body, mesh=mesh, in_specs=placed, out_specs=P("tm", "dom"), check_vma=False
    )
```
